256 devices in a mesh: seq: 64 (over x, y, z_hi), tp: 4 (over z_lo, core).
Axes of the slice: x: 4, y: 4, z: 8 (z_hi: 4, z_lo: 2; z = z_hi * 2 + z_lo), core: 2. Of those that a mesh axis runs over, the one named last changes fastest.
Arguments:
- queries: bfloat16 [2, 4096, 2560], P(None, 'seq', 'tp'), may hold values from -8 to 8
- keys: bfloat16 [2, 4096, 2560], P(None, 'seq', 'tp'), may hold values from -4.5 to 4.5
- values: bfloat16 [2, 4096, 2560], P(None, 'seq', 'tp'), may hold values from -48 to 48
- queries_tan: bfloat16 [2, 4096, 2560], P(None, 'seq', 'tp'), may hold values from -6 to 6
- keys_tan: bfloat16 [2, 4096, 2560], P(None, 'seq', 'tp'), may hold values from -6 to 6
- values_tan: bfloat16 [2, 4096, 2560], P(None, 'seq', 'tp'), may hold values from -48 to 48
- w_out: bfloat16 [2560, 5120], P('tp'), may hold values from -0.125 to 0.125
- grad_out: bfloat16 [2, 4096, 5120], P(None, 'seq', 'tp'), may hold values from -24 to 24
Outputs:
- out: bfloat16 [2, 4096, 5120], P(None, 'seq', 'tp')
- out_tan: bfloat16 [2, 4096, 5120], P(None, 'seq', 'tp')
- grad_queries: bfloat16 [2, 4096, 2560], P(None, 'seq', 'tp')
- grad_keys: bfloat16 [2, 4096, 2560], P(None, 'seq', 'tp')
- grad_values: bfloat16 [2, 4096, 2560], P(None, 'seq', 'tp')
The draws below stay inside these ranges and needn't reach their ends.
All inputs are finite; a program needn't handle non-finite values.
Results may differ from the reference program's by a relative error of at most 0.035.
Values may be sent and summed in bfloat16 or wider, within the bound.
No kernel may reach another device: no remote copies, remote signals or barrier semaphores. Data moves between devices by JAX's collectives and lax.ppermute only.
A program may use at most 192 MiB of HBM per device.

```python
import jax
import jax.numpy as jnp
from jax import lax

D = 5120
HEADS = 20
HD = 128
SEQS = 2
TOKENS = 4096


def draw_queries(key, part):
    key = jax.random.fold_in(key, 1)
    base = jnp.clip(2.0 * jax.random.normal(key, (SEQS, TOKENS, HEADS * HD)), -8.0, 8.0)
    return base.astype(jnp.bfloat16)


def draw_keys(key, part):
    key = jax.random.fold_in(key, 2)
    base = jnp.clip(jax.random.normal(key, (SEQS, TOKENS, HEADS * HD)), -4.5, 4.5)
    return base.astype(jnp.bfloat16)


def level_of(own_key, extent, split, low, top_value):
    def one(position, shards_of):
        heights = jax.random.uniform(jax.random.fold_in(jax.random.fold_in(own_key, 6), position), (shards_of,), jnp.float32, low / len(split), top_value / len(split))
        return jnp.repeat(jnp.exp(heights), extent[position] // shards_of).reshape((-1,) + (1,) * (len(extent) - position - 1))

    loudness = one(*split[0])
    for cut in split[1:]:
        loudness = loudness * one(*cut)
    return loudness


def scatter_about(own_key, shape, width, limit, shards=(), dtype=jnp.bfloat16):
    result = jax.random.normal(own_key, shape, jnp.float32) * width
    if len(shards) > 0:
        result = level_of(own_key, shape, shards, -0.22, 0.18) * result
    return jnp.clip(result, min=-limit, max=limit).astype(dtype)


def setup_inputs(seed: int = 0) -> dict:
    arg_keys = jax.random.split(jax.random.key(seed), 9)
    return {
        "queries": draw_queries(jax.random.fold_in(arg_keys[8], 71), 0),
        "keys": draw_keys(jax.random.fold_in(arg_keys[8], 71), 0),
        "values": scatter_about(arg_keys[2], (SEQS, TOKENS, HEADS * HD), 8.0, 48.0, ((1, 64), (2, 4))),
        "queries_tan": scatter_about(arg_keys[3], (SEQS, TOKENS, HEADS * HD), 1.0, 6.0, ((1, 64), (2, 4))),
        "keys_tan": scatter_about(arg_keys[4], (SEQS, TOKENS, HEADS * HD), 1.0, 6.0, ((1, 64), (2, 4))),
        "values_tan": scatter_about(arg_keys[5], (SEQS, TOKENS, HEADS * HD), 8.0, 48.0, ((1, 64), (2, 4))),
        "w_out": scatter_about(arg_keys[6], (HEADS * HD, D), (HEADS * HD) ** -0.5, 0.125, ((0, 4),)),
        "grad_out": scatter_about(arg_keys[7], (SEQS, TOKENS, D), 4.0, 24.0, ((1, 64), (2, 4))),
    }


def matmul(left, right):
    return jnp.dot(left.astype(jnp.float32), right.astype(jnp.float32), precision=lax.Precision.HIGHEST, preferred_element_type=jnp.float32)


def one_head(inputs):
    query, key_rows, value, query_tan, key_tan, value_tan, cot = inputs
    scale = HD ** -0.5
    scores = scale * matmul(query, key_rows.T)
    slopes = scale * (matmul(query_tan, key_rows.T) + matmul(query, key_tan.T))
    top = jnp.max(scores, axis=-1, keepdims=True)
    lse = top + jnp.log(jnp.sum(jnp.exp(scores - top), axis=-1, keepdims=True))
    probs = jnp.exp(scores - lse)
    probs_b = probs.astype(jnp.bfloat16)
    attn = matmul(probs_b, value).astype(jnp.bfloat16)
    mean_slope = jnp.sum(probs * slopes, axis=-1, keepdims=True)
    weights_t = (probs * (slopes - mean_slope)).astype(jnp.bfloat16)
    attn_tan = (matmul(weights_t, value) + matmul(probs_b, value_tan)).astype(jnp.bfloat16)
    dsum = jnp.sum(cot.astype(jnp.float32) * attn.astype(jnp.float32), axis=-1, keepdims=True)
    dscore = (probs * (matmul(cot, value.T) - dsum)).astype(jnp.bfloat16)
    grad_q = (scale * matmul(dscore, key_rows)).astype(jnp.bfloat16)
    grad_k = (scale * matmul(dscore.T, query)).astype(jnp.bfloat16)
    grad_v = matmul(probs_b.T, cot).astype(jnp.bfloat16)
    return attn, attn_tan, grad_q, grad_k, grad_v


def heads_first(array):
    return array.reshape(TOKENS, HEADS, HD).transpose(1, 0, 2)


def heads_last(array):
    return array.transpose(1, 0, 2).reshape(TOKENS, HEADS * HD)


def one_clip(inputs):
    queries, keys, values, queries_tan, keys_tan, values_tan, grad_out, w_out = inputs
    cot = jnp.dot(grad_out, w_out.T, preferred_element_type=jnp.float32).astype(jnp.bfloat16)
    stacked = tuple(heads_first(a) for a in (queries, keys, values, queries_tan, keys_tan, values_tan, cot))
    attn, attn_tan, grad_q, grad_k, grad_v = lax.map(one_head, stacked)
    attn = heads_last(attn)
    attn_tan = heads_last(attn_tan)
    out = jnp.dot(attn, w_out, preferred_element_type=jnp.float32).astype(jnp.bfloat16)
    out_tan = jnp.dot(attn_tan, w_out, preferred_element_type=jnp.float32).astype(jnp.bfloat16)
    return out, out_tan, heads_last(grad_q), heads_last(grad_k), heads_last(grad_v)


def reference(queries, keys, values, queries_tan, keys_tan, values_tan, w_out, grad_out):
    weights = jnp.broadcast_to(w_out[None], (SEQS,) + w_out.shape)
    out, out_tan, grad_q, grad_k, grad_v = lax.map(one_clip, (queries, keys, values, queries_tan, keys_tan, values_tan, grad_out, weights))
    return out, out_tan, grad_q, grad_k, grad_v
```

```python
import jax
import jax.numpy as jnp
from jax import lax
from jax.experimental import pallas as pl
from jax.experimental.pallas import tpu as pltpu
from jax.sharding import Mesh, PartitionSpec as P

HD = 128
SCALE = HD ** (-0.5)
LOG2E = 1.4426950408889634
TILE = 256
SRC = 4
NT = (((1,), (1,)), ((), ()))
NN = (((1,), (0,)), ((), ()))


def dot(a, b, dims=NN):
    return lax.dot_general(a, b, dims, preferred_element_type=jnp.float32)


def attention_kernel(q_ref, ka_ref, kb_ref, oq_ref, oa_ref, ob_ref, s_scr, t_scr, d_scr, vt_scr, kt_scr, g_scr):
    step = pl.program_id(0)
    blocks, rows = ka_ref.shape[0], ka_ref.shape[1]
    chunk = SRC * rows
    per = blocks // SRC
    qtq = q_ref[:, 0:2 * HD]
    q = q_ref[:, HD:2 * HD]
    g = q_ref[:, 2 * HD:3 * HD]

    def load(ref, j, lo, hi):
        return ref[pl.ds(j * SRC, SRC), :, lo * HD:hi * HD].reshape(chunk, (hi - lo) * HD)

    def at(half, j):
        return pl.ds(pl.multiple_of((half * per + j) * chunk, chunk), chunk)

    @pl.when(step == 0)
    def _():
        for half, ref in enumerate((ka_ref, kb_ref)):
            def body(j, carry):
                vt_scr[:, at(half, j)] = load(ref, j, 2, 4).T
                kt_scr[:, at(half, j)] = load(ref, j, 0, 1).T
                return carry
            lax.fori_loop(0, per, body, 0)
        g_scr[...] = jnp.zeros_like(g_scr)

    top = jnp.full((1, TILE), -jnp.inf, jnp.float32)
    for half, ref in enumerate((ka_ref, kb_ref)):
        def body(j, top):
            s = dot(load(ref, j, 0, 1), q, NT)
            s_scr[at(half, j), :] = s
            t_scr[at(half, j), :] = dot(load(ref, j, 0, 2), qtq, NT)
            d_scr[at(half, j), :] = dot(load(ref, j, 2, 3), g, NT)
            return jnp.maximum(top, jnp.max(s, axis=0, keepdims=True))
        top = lax.fori_loop(0, per, body, top)

    zero = jnp.zeros((1, TILE), jnp.float32)
    def body(j, carry):
        total, slope, dsum = carry
        rows_at = at(0, j)
        e = jnp.exp2((s_scr[rows_at, :] - top) * (SCALE * LOG2E))
        s_scr[rows_at, :] = e
        total += jnp.sum(e, axis=0, keepdims=True)
        slope += jnp.sum(e * t_scr[rows_at, :], axis=0, keepdims=True)
        dsum += jnp.sum(e * d_scr[rows_at, :], axis=0, keepdims=True)
        return total, slope, dsum
    total, slope, dsum = lax.fori_loop(0, 2 * per, body, (zero, zero, zero))
    inv = 1.0 / total
    slope = slope * inv
    dsum = dsum * inv

    acc = (jnp.zeros((2 * HD, TILE), jnp.float32), jnp.zeros((HD, TILE), jnp.float32), jnp.zeros((HD, TILE), jnp.float32))
    def body(j, carry):
        att, tan, dq = carry
        rows_at = at(0, j)
        p = s_scr[rows_at, :] * inv
        pb = p.astype(jnp.bfloat16)
        w = (p * (t_scr[rows_at, :] - slope)).astype(jnp.bfloat16)
        ds = (p * (d_scr[rows_at, :] - dsum)).astype(jnp.bfloat16)
        att += dot(vt_scr[:, rows_at], pb)
        tan += dot(vt_scr[0:HD, rows_at], w)
        dq += dot(kt_scr[:, rows_at], ds)
        g_scr[rows_at, 0:HD] += dot(ds, q)
        g_scr[rows_at, HD:2 * HD] += dot(pb, g)
        return att, tan, dq
    att, tan, dq = lax.fori_loop(0, 2 * per, body, acc)
    oq_ref[:, 0:HD] = att[0:HD].T.astype(jnp.bfloat16)
    oq_ref[:, HD:2 * HD] = (att[HD:] + SCALE * tan).T.astype(jnp.bfloat16)
    oq_ref[:, 2 * HD:3 * HD] = (SCALE * dq).T.astype(jnp.bfloat16)

    @pl.when(step == pl.num_programs(0) - 1)
    def _():
        for half, ref in enumerate((oa_ref, ob_ref)):
            def body(j, carry):
                block = g_scr[at(half, j), :]
                ref[pl.ds(j * SRC, SRC), :, 0:HD] = (SCALE * block[:, 0:HD]).astype(jnp.bfloat16).reshape(SRC, rows, HD)
                ref[pl.ds(j * SRC, SRC), :, HD:2 * HD] = block[:, HD:].astype(jnp.bfloat16).reshape(SRC, rows, HD)
                return carry
            lax.fori_loop(0, per, body, 0)


def attention(q_side, own, other):
    n = q_side.shape[0]
    blocks, rows, _ = own.shape
    keys = 2 * blocks * rows
    whole = lambda a: pl.BlockSpec(a.shape, lambda i: (0,) * len(a.shape))
    grads = jax.ShapeDtypeStruct((blocks, rows, 2 * HD), jnp.bfloat16)
    return pl.pallas_call(
        attention_kernel,
        grid=(n // TILE,),
        in_specs=[pl.BlockSpec((TILE, 3 * HD), lambda i: (i, 0)), whole(own), whole(other)],
        out_specs=[pl.BlockSpec((TILE, 3 * HD), lambda i: (i, 0)), whole(grads), whole(grads)],
        out_shape=[jax.ShapeDtypeStruct((n, 3 * HD), jnp.bfloat16), grads, grads],
        scratch_shapes=[
            pltpu.VMEM((keys, TILE), jnp.float32),
            pltpu.VMEM((keys, TILE), jnp.float32),
            pltpu.VMEM((keys, TILE), jnp.float32),
            pltpu.VMEM((2 * HD, keys), jnp.bfloat16),
            pltpu.VMEM((HD, keys), jnp.bfloat16),
            pltpu.VMEM((keys, 2 * HD), jnp.float32),
        ],
        compiler_params=pltpu.CompilerParams(vmem_limit_bytes=56 * 2**20, dimension_semantics=("arbitrary",)),
        cost_estimate=pl.CostEstimate(flops=20 * n * keys * HD, bytes_accessed=10 * 2**20, transcendentals=n * keys),
    )(q_side, own, other)


SWAP = [(0, 1), (1, 0)]
THIRDS = 3
OVERLAP = 8


def swap(array, axis):
    return lax.ppermute(array, axis, SWAP)


def pair(mine, theirs, index, axis):
    first = jnp.where(index == 0, mine, theirs)
    second = jnp.where(index == 0, theirs, mine)
    return jnp.concatenate([first, second], axis=axis)


def gather_features(grad, w, c):
    far = swap(grad, "w")
    near = swap(grad, "c")
    far_near = swap(far, "c")
    return pair(pair(grad, near, c, 2), pair(far, far_near, c, 2), w, 2)


def scatter_features(partial, w, c):
    rows = partial.shape[0]
    split = partial.reshape(rows, 2, 2, -1)
    mine = lax.dynamic_index_in_dim(split, c, 2, keepdims=False)
    theirs = lax.dynamic_index_in_dim(split, 1 - c, 2, keepdims=False)
    half = (mine + swap(theirs.astype(jnp.bfloat16), "c").astype(jnp.float32))
    keep = lax.dynamic_index_in_dim(half, w, 1, keepdims=False)
    give = lax.dynamic_index_in_dim(half, 1 - w, 1, keepdims=False)
    got = swap(give.astype(jnp.bfloat16), "w")
    return (keep + got.astype(jnp.float32)).astype(jnp.bfloat16)


def to_plane(packed):
    clips, tokens, width = packed.shape
    halves = packed.reshape(clips, 2, tokens // 2, width).transpose(1, 0, 2, 3)
    near = lax.all_to_all(halves, "c", 0, 0, tiled=True)
    slots = near.reshape(2 * clips, tokens // 2, width)
    return lax.all_to_all(slots, "z", 0, 0, tiled=True).reshape(-1, width)


def from_plane(packed, clips):
    rows, width = packed.shape
    slots = packed.reshape(2 * clips, rows // (2 * clips), width)
    back = lax.all_to_all(slots, "z", 0, 0, tiled=True).reshape(2, clips, -1, width)
    halves = lax.all_to_all(back, "c", 0, 0, tiled=True)
    return halves.transpose(1, 0, 2, 3).reshape(clips, -1, width)


def chips(array):
    heads, thirds = array.shape[:2]
    flat = array.reshape((heads * thirds,) + array.shape[2:])
    count = lax.axis_size(("x", "y"))
    pad = jnp.zeros((count - heads * thirds,) + flat.shape[1:], flat.dtype)
    return jnp.concatenate([flat, pad], axis=0)


def over_chips(array):
    return lax.all_to_all(array, ("x", "y"), 0, 0, tiled=True)


def local(queries, keys, values, queries_tan, keys_tan, values_tan, w_out, grad_out):
    w, c = lax.axis_index("w"), lax.axis_index("c")
    clips, tokens, features = queries.shape
    heads = features // HD

    full_grad = gather_features(grad_out, w, c)
    cot = jnp.einsum("btf,cf->btc", full_grad, w_out, preferred_element_type=jnp.float32).astype(
        jnp.bfloat16
    )

    kinds = (keys, keys_tan, values, values_tan, queries_tan, queries, cot)
    packed = jnp.stack([a.reshape(clips, tokens, heads, HD) for a in kinds], axis=3)
    plane = to_plane(packed.reshape(clips, tokens, -1))
    plane = plane.reshape(-1, heads, 7 * HD).transpose(1, 0, 2)
    rows = plane.shape[1]

    key_side = plane[:, None, :, 0:4 * HD]
    own = over_chips(chips(jnp.broadcast_to(key_side, (heads, THIRDS) + key_side.shape[2:])))
    other = swap(own, "c")

    query_side = plane[:, :, 4 * HD:7 * HD]
    step = (rows - OVERLAP) // THIRDS
    window = step + OVERLAP
    first = lax.broadcasted_iota(jnp.int32, (1, window, 3 * HD), 1) < OVERLAP
    is_cot = lax.broadcasted_iota(jnp.int32, (1, window, 3 * HD), 2) >= 2 * HD
    windows = []
    for third in range(THIRDS):
        piece = query_side[:, third * step:third * step + window]
        if third > 0:
            piece = jnp.where(first & is_cot, jnp.zeros_like(piece), piece)
        windows.append(piece)
    q_recv = over_chips(chips(jnp.stack(windows, axis=1)))

    oq, own_grads, other_grads = attention(q_recv.reshape(-1, 3 * HD), own, other)

    got = swap(other_grads, "c")
    grads = (own_grads.astype(jnp.float32) + got.astype(jnp.float32)).astype(jnp.bfloat16)
    q_back = over_chips(oq.reshape(q_recv.shape))[:heads * THIRDS]
    k_back = over_chips(grads)[:heads * THIRDS]

    q_back = q_back.reshape(heads, THIRDS, window, 3 * HD)
    q_done = jnp.concatenate(
        [q_back[:, 0]] + [q_back[:, third, OVERLAP:] for third in range(1, THIRDS)], axis=1
    )
    k_back = k_back.reshape(heads, THIRDS, rows, 2 * HD).astype(jnp.float32)
    k_done = jnp.sum(k_back, axis=1).astype(jnp.bfloat16)
    done = jnp.concatenate([q_done, k_done], axis=2).transpose(1, 0, 2)
    home = from_plane(done.reshape(rows, -1), clips).reshape(clips, tokens, heads, 5, HD)
    attn, attn_tan, grad_q, grad_k, grad_v = (
        home[:, :, :, i].reshape(clips, tokens, features) for i in range(5)
    )

    both = jnp.concatenate([attn, attn_tan], axis=0).reshape(-1, features)
    partial = jnp.dot(both, w_out, preferred_element_type=jnp.float32)
    outs = scatter_features(partial, w, c).reshape(2, clips, tokens, -1)
    return outs[0], outs[1], grad_q, grad_k, grad_v


def solution(mesh):
    seq, tp = ("x", "y", "z"), ("w", "c")
    fine = Mesh(mesh.devices.reshape(4, 4, 4, 2, 2), seq + tp)
    split = P(None, seq, tp)
    return jax.shard_map(
        local,
        mesh=fine,
        in_specs=(split,) * 6 + (P(tp, None), split),
        out_specs=(split,) * 5,
        check_vma=False,
    )
```

```python
import functools

import jax
import jax.numpy as jnp
from jax import lax
from jax.experimental import pallas as pl
from jax.experimental.pallas import tpu as pltpu
from jax.sharding import Mesh, PartitionSpec as P

HD = 128
SCALE = HD ** (-0.5)
LOG2E = 1.4426950408889634
SUB = 16
SRC = 4
NT = (((1,), (1,)), ((), ()))
NN = (((1,), (0,)), ((), ()))


def dot(a, b, dims=NN):
    return lax.dot_general(a, b, dims, preferred_element_type=jnp.float32)


def piece(ref, j, first, count, lanes=slice(None)):
    block = ref[pl.ds(j * SRC, SRC), first:first + count, lanes]
    return block.reshape(SRC * count, block.shape[-1])


def key_rows(half, j, blocks, rows):
    start = (half * blocks + j * SRC) * rows
    return pl.ds(pl.multiple_of(start, SRC * rows), SRC * rows)


def weights_kernel(rows, z_ref, q_ref, ka_ref, kb_ref, p_ref, w_ref, s_scr, t_scr):
    blocks = ka_ref.shape[0]
    tile = p_ref.shape[1]
    qtq = q_ref[...].reshape(tile, 2 * HD)
    q = qtq[:, HD:]

    top = jnp.full((1, tile), -jnp.inf, jnp.float32)
    for half, ref in enumerate((ka_ref, kb_ref)):
        def scores(j, top, half=half, ref=ref):
            here = key_rows(half, j, blocks, rows)
            both = piece(ref, j, 0, rows)
            s = dot(both[:, :HD], q, NT)
            s_scr[here, :] = s
            t_scr[here, :] = dot(both, qtq, NT)
            return jnp.maximum(top, jnp.max(s, axis=0, keepdims=True))
        top = lax.fori_loop(0, blocks // SRC, scores, top)

    zero = jnp.zeros((1, tile), jnp.float32)

    def sums(j, carry):
        total, slope = carry
        here = key_rows(0, j, blocks, rows)
        e = jnp.exp2((s_scr[here, :] - top) * (SCALE * LOG2E))
        s_scr[here, :] = e
        total += jnp.sum(e, axis=0, keepdims=True)
        slope += jnp.sum(e * t_scr[here, :], axis=0, keepdims=True)
        return total, slope

    total, slope = lax.fori_loop(0, 2 * blocks // SRC, sums, (zero, zero))
    inv = 1.0 / total
    slope = slope * inv

    def store(j, carry):
        here = key_rows(0, j, blocks, rows)
        p = s_scr[here, :] * inv
        p_ref[here, :] = p.astype(jnp.bfloat16)
        w_ref[here, :] = (p * (t_scr[here, :] - slope)).astype(jnp.bfloat16)
        return carry

    lax.fori_loop(0, 2 * blocks // SRC, store, 0)


def values_kernel(rows, z_ref, g_ref, va_ref, vb_ref, p_ref, w_ref, out_ref, d_ref, vt_scr):
    blocks = va_ref.shape[0]
    tile = p_ref.shape[1]

    @pl.when(pl.program_id(0) == 0)
    def _():
        for half, ref in enumerate((va_ref, vb_ref)):
            def turn(j, carry, half=half, ref=ref):
                here = key_rows(half, j, blocks, rows)
                vt_scr[0:HD, here] = piece(ref, j, 0, rows).T
                vt_scr[HD:, here] = piece(ref, j, rows, rows).T
                return carry
            lax.fori_loop(0, blocks // SRC, turn, 0)

    def add(j, carry):
        both, tan = carry
        here = key_rows(0, j, blocks, rows)
        both += dot(vt_scr[:, here], p_ref[here, :])
        tan += dot(vt_scr[0:HD, here], w_ref[here, :])
        return both, tan

    zeros = jnp.zeros((2 * HD, tile), jnp.float32), jnp.zeros((HD, tile), jnp.float32)
    both, tan = lax.fori_loop(0, 2 * blocks // SRC, add, zeros)
    attn = both[0:HD].astype(jnp.bfloat16)
    g = g_ref[...].reshape(tile, HD)
    d_ref[...] = jnp.sum(attn.astype(jnp.float32) * g.astype(jnp.float32).T, axis=0, keepdims=True)
    out_ref[:, :, 0:HD] = both[0:HD].T.astype(jnp.bfloat16).reshape(-1, SUB, HD)
    out_ref[:, :, HD:] = (both[HD:] + SCALE * tan).T.astype(jnp.bfloat16).reshape(-1, SUB, HD)


def grads_kernel(rows, z_ref, q_ref, g_ref, ka_ref, kb_ref, va_ref, vb_ref, p_ref, d_ref, dq_ref, oa_ref, ob_ref, kt_scr, k_scr, v_scr):
    blocks = ka_ref.shape[0]
    tile = p_ref.shape[1]
    step = pl.program_id(0)
    q = q_ref[...].reshape(tile, 2 * HD)[:, HD:]
    g = g_ref[...].reshape(tile, HD)
    dsum = d_ref[...]

    @pl.when(step == 0)
    def _():
        for half, ref in enumerate((ka_ref, kb_ref)):
            def turn(j, carry, half=half, ref=ref):
                kt_scr[:, key_rows(half, j, blocks, rows)] = piece(ref, j, 0, rows, slice(0, HD)).T
                return carry
            lax.fori_loop(0, blocks // SRC, turn, 0)
        k_scr[...] = jnp.zeros_like(k_scr)
        v_scr[...] = jnp.zeros_like(v_scr)

    dq = jnp.zeros((HD, tile), jnp.float32)
    for half, ref in enumerate((va_ref, vb_ref)):
        def add(j, dq, half=half, ref=ref):
            here = key_rows(half, j, blocks, rows)
            p = p_ref[here, :]
            slopes = dot(piece(ref, j, 0, rows), g, NT) - dsum
            ds = (p.astype(jnp.float32) * slopes).astype(jnp.bfloat16)
            k_scr[here, :] += dot(ds, q)
            v_scr[here, :] += dot(p, g)
            return dq + dot(kt_scr[:, here], ds)
        dq = lax.fori_loop(0, blocks // SRC, add, dq)
    dq_ref[...] = (SCALE * dq).T.astype(jnp.bfloat16).reshape(-1, SUB, HD)

    @pl.when(step == pl.num_programs(0) - 1)
    def _():
        for half, ref in enumerate((oa_ref, ob_ref)):
            def give(j, carry, half=half, ref=ref):
                here = key_rows(half, j, blocks, rows)
                group = pl.ds(j * SRC, SRC)
                ref[group, 0:rows, :] = (SCALE * k_scr[here, :]).astype(jnp.bfloat16).reshape(SRC, rows, HD)
                ref[group, rows:, :] = v_scr[here, :].astype(jnp.bfloat16).reshape(SRC, rows, HD)
                return carry
            lax.fori_loop(0, blocks // SRC, give, 0)


def whole(array):
    return pl.BlockSpec(array.shape, lambda i, s: (0,) * len(array.shape))


def kernel_call(body, name, grid, scalars, ins, outs, scratch, flops=0, bytes_accessed=4 * 2**20):
    arrays, in_specs = zip(*ins)
    shapes, out_specs = zip(*outs)
    return pl.pallas_call(
        body,
        grid_spec=pltpu.PrefetchScalarGridSpec(
            num_scalar_prefetch=1,
            grid=(grid,),
            in_specs=list(in_specs),
            out_specs=list(out_specs),
            scratch_shapes=scratch,
        ),
        out_shape=list(shapes),
        name=name,
        compiler_params=pltpu.CompilerParams(vmem_limit_bytes=52 * 2**20),
        cost_estimate=pl.CostEstimate(flops=flops, bytes_accessed=bytes_accessed, transcendentals=0),
    )(scalars, *arrays)


def specs(blocks, rows, window):
    tile = blocks * SUB
    keys = 2 * blocks * rows
    q_spec = pl.BlockSpec((blocks, SUB, 2 * HD), lambda i, s: (0, rows // SUB + i, 0))
    g_spec = pl.BlockSpec((blocks, SUB, HD), lambda i, s: (0, 2 * rows // SUB + i, 0))
    p_spec = pl.BlockSpec((keys, tile), lambda i, s: (0, i))
    d_spec = pl.BlockSpec((1, tile), lambda i, s: (0, i))
    return q_spec, g_spec, p_spec, d_spec, keys, tile, window // SUB


def attention_weights(z, recv_k, other_k, rows, window):
    q_spec, _, p_spec, _, keys, tile, grid = specs(recv_k.shape[0], rows, window)
    p_shape = jax.ShapeDtypeStruct((keys, grid * tile), jnp.bfloat16)
    return kernel_call(
        functools.partial(weights_kernel, rows), "weights", grid, z,
        [(recv_k, q_spec), (recv_k, whole(recv_k)), (other_k, whole(other_k))],
        [(p_shape, p_spec), (p_shape, p_spec)],
        [pltpu.VMEM((keys, tile), jnp.float32), pltpu.VMEM((keys, tile), jnp.float32)],
        8 * keys * grid * tile * HD, 32 * 2**20)


def attention_values(z, recv_v, other_v, probs, weights, rows, window):
    blocks = recv_v.shape[0]
    _, g_spec, p_spec, d_spec, keys, tile, grid = specs(blocks, rows, window)
    out_shape = jax.ShapeDtypeStruct((blocks, window, 2 * HD), jnp.bfloat16)
    d_shape = jax.ShapeDtypeStruct((1, grid * tile), jnp.float32)
    return kernel_call(
        functools.partial(values_kernel, rows), "values", grid, z,
        [(recv_v, g_spec), (recv_v, whole(recv_v)), (other_v, whole(other_v)), (probs, p_spec), (weights, p_spec)],
        [(out_shape, pl.BlockSpec((blocks, SUB, 2 * HD), lambda i, s: (0, i, 0))), (d_shape, d_spec)],
        [pltpu.VMEM((2 * HD, keys), jnp.bfloat16)],
        6 * keys * grid * tile * HD, 16 * 2**20)


def attention_grads(z, recv_k, other_k, recv_v, other_v, probs, dsum, rows, window):
    blocks = recv_v.shape[0]
    q_spec, g_spec, p_spec, d_spec, keys, tile, grid = specs(blocks, rows, window)
    dq_shape = jax.ShapeDtypeStruct((blocks, window, HD), jnp.bfloat16)
    shape = jax.ShapeDtypeStruct((blocks, 2 * rows, HD), jnp.bfloat16)
    return kernel_call(
        functools.partial(grads_kernel, rows), "grads", grid, z,
        [(recv_k, q_spec), (recv_v, g_spec), (recv_k, whole(recv_k)), (other_k, whole(other_k)),
         (recv_v, whole(recv_v)), (other_v, whole(other_v)), (probs, p_spec), (dsum, d_spec)],
        [(dq_shape, pl.BlockSpec((blocks, SUB, HD), lambda i, s: (0, i, 0))),
         (shape, whole(shape)), (shape, whole(shape))],
        [pltpu.VMEM((HD, keys), jnp.bfloat16), pltpu.VMEM((keys, HD), jnp.float32), pltpu.VMEM((keys, HD), jnp.float32)],
        10 * keys * grid * tile * HD, 32 * 2**20)


THIRDS = 3
SWAP = [(0, 1), (1, 0)]


def swap(array, axis):
    return lax.ppermute(array, axis, SWAP)


def plane_routes(planes):
    routes = []
    for d in range(planes):
        route = []
        for z in range(planes):
            for c in range(2):
                slot = (z + d) % planes
                route.append((z * 2 + c, (2 * c + slot // 2) * 2 + slot % 2))
        routes.append(route)
    return routes


def to_plane(pieces):
    return [lax.ppermute(a, ("z", "c"), route) for a, route in zip(pieces, plane_routes(len(pieces)))]


def from_plane(pieces):
    routes = plane_routes(len(pieces))
    return [lax.ppermute(a, ("z", "c"), [(b, a) for a, b in route]) for a, route in zip(pieces, routes)]


def over_chips(array):
    return lax.all_to_all(array, ("x", "y"), 0, 0, tiled=True)


def slot_of(z_ref, d, count):
    slot = lax.rem(z_ref[0] + d, count)
    return slot // 2, lax.rem(slot, 2)


def split_kernel(kinds, z_ref, *refs):
    outs = refs[kinds:]
    _, tokens, width = refs[0].shape
    half_rows = tokens // 2
    for d, out in enumerate(outs):
        clip, half = slot_of(z_ref, d, len(outs))
        for index, ref in enumerate(refs[:kinds]):
            start = pl.multiple_of(half * half_rows, half_rows)
            out[:, index * width:(index + 1) * width] = ref[clip, pl.ds(start, half_rows), :]


def split_slots(name, z, arrays):
    clips, tokens, width = arrays[0].shape
    shape = jax.ShapeDtypeStruct((tokens // 2, len(arrays) * width), jnp.bfloat16)
    return kernel_call(
        functools.partial(split_kernel, len(arrays)), name, 1, z,
        [(a, whole(a)) for a in arrays], [(shape, whole(shape))] * (2 * clips), [])


def join_kernel(kinds, z_ref, *refs):
    ins, outs = refs[:-kinds], refs[-kinds:]
    half_rows = ins[0].shape[0]
    width = outs[0].shape[2]
    for d, ref in enumerate(ins):
        clip, half = slot_of(z_ref, d, len(ins))
        for index, out in enumerate(outs):
            start = pl.multiple_of(half * half_rows, half_rows)
            out[clip, pl.ds(start, half_rows), :] = ref[:, index * width:(index + 1) * width]


def join_slots(name, z, pieces, kinds, clips):
    rows, width = pieces[0].shape
    shape = jax.ShapeDtypeStruct((clips, 2 * rows, width // kinds), jnp.bfloat16)
    return kernel_call(
        functools.partial(join_kernel, kinds), name, 1, z,
        [(a, whole(a)) for a in pieces], [(shape, whole(shape))] * kinds, [])


def keys_kernel(heads, z_ref, *refs):
    ins, out = refs[:-1], refs[-1]
    part = ins[0].shape[0]
    rows = part * len(ins)
    window = out.shape[1] - rows
    width = heads * HD
    for head in range(heads):
        for kind in range(4):
            source = slice(kind * width + head * HD, kind * width + (head + 1) * HD)
            lanes = slice((kind % 2) * HD, (kind % 2 + 1) * HD)
            whole_block = jnp.concatenate([ref[:, source] for ref in ins], axis=0)
            for third in range(THIRDS):
                chip = head * THIRDS + third
                if kind < 2:
                    out[chip, 0:rows, lanes] = whole_block
                else:
                    first = third * window
                    count = min(window, rows - first)
                    out[chip, rows:rows + count, lanes] = whole_block[first:first + count]
                    if count < window:
                        out[chip, rows + count:, lanes] = jnp.zeros((window - count, HD), out.dtype)
    for chip in range(heads * THIRDS, out.shape[0]):
        out[chip] = jnp.zeros(out.shape[1:], out.dtype)


def values_pack_kernel(heads, z_ref, *refs):
    ins, out = refs[:-1], refs[-1]
    rows = ins[0].shape[0] * len(ins)
    window = out.shape[1] - 2 * rows
    width = heads * HD
    for head in range(heads):
        for kind in range(3):
            source = slice(kind * width + head * HD, kind * width + (head + 1) * HD)
            whole_block = jnp.concatenate([ref[:, source] for ref in ins], axis=0)
            for third in range(THIRDS):
                chip = head * THIRDS + third
                if kind < 2:
                    out[chip, kind * rows:(kind + 1) * rows, :] = whole_block
                else:
                    first = third * window
                    count = min(window, rows - first)
                    out[chip, 2 * rows:2 * rows + count, :] = whole_block[first:first + count]
                    if count < window:
                        out[chip, 2 * rows + count:, :] = jnp.zeros((window - count, HD), out.dtype)
    for chip in range(heads * THIRDS, out.shape[0]):
        out[chip] = jnp.zeros(out.shape[1:], out.dtype)


def out_unpack_kernel(heads, z_ref, back_ref, *outs):
    part = outs[0].shape[0]
    window = back_ref.shape[1]
    rows = part * len(outs)
    width = heads * HD
    for head in range(heads):
        for kind in range(2):
            lanes = slice(kind * HD, (kind + 1) * HD)
            pieces = [
                back_ref[head * THIRDS + third, 0:min(window, rows - third * window), lanes]
                for third in range(THIRDS)
            ]
            column = jnp.concatenate(pieces, axis=0)
            for d, out in enumerate(outs):
                out[:, kind * width + head * HD:kind * width + (head + 1) * HD] = column[d * part:(d + 1) * part]


def grads_unpack_kernel(heads, z_ref, back_ref, *outs):
    part = outs[0].shape[0]
    rows = part * len(outs)
    window = back_ref.shape[1] - 2 * rows
    width = heads * HD
    for head in range(heads):
        for kind in range(3):
            chips = [head * THIRDS + third for third in range(THIRDS)]
            if kind < 2:
                column = sum(
                    back_ref[chip, kind * rows:(kind + 1) * rows, :].astype(jnp.float32) for chip in chips
                ).astype(jnp.bfloat16)
            else:
                column = jnp.concatenate([
                    back_ref[chip, 2 * rows:2 * rows + min(window, rows - third * window), :]
                    for third, chip in enumerate(chips)
                ], axis=0)
            for d, out in enumerate(outs):
                out[:, kind * width + head * HD:kind * width + (head + 1) * HD] = column[d * part:(d + 1) * part]


def merge_kernel(z_ref, own_ref, got_ref, dq_ref, out_ref):
    rows = got_ref.shape[1]
    total = own_ref[...].astype(jnp.float32) + got_ref[...].astype(jnp.float32)
    out_ref[:, 0:rows, :] = total.astype(jnp.bfloat16)
    out_ref[:, rows:, :] = dq_ref[...]


def repack(body, name, z, ins, shapes):
    shapes = [jax.ShapeDtypeStruct(s, jnp.bfloat16) for s in shapes]
    return kernel_call(body, name, 1, z, [(a, whole(a)) for a in ins], [(s, whole(s)) for s in shapes], [])


def local(queries, keys, values, queries_tan, keys_tan, values_tan, w_out, grad_out):
    w, c = lax.axis_index("w"), lax.axis_index("c")
    z = lax.axis_index("z").astype(jnp.int32).reshape(1)
    clips, tokens, features = queries.shape
    heads = features // HD
    chips = lax.axis_size(("x", "y"))
    slots = 2 * clips
    rows = slots * tokens // 2
    window = pl.cdiv(pl.cdiv(rows, THIRDS), SUB) * SUB

    far = swap(grad_out, "w")
    near = swap(grad_out, "c")
    split = split_slots("split_keys", z, (keys, keys_tan, queries_tan, queries))
    split, far = lax.optimization_barrier((split, far))
    plane = to_plane(split)
    cross = swap(far, "c")
    width = grad_out.shape[2]
    w_own, w_near, w_far, w_cross = blocks = [
        lax.dynamic_slice_in_dim(w_out, ((w ^ i) * 2 + (c ^ j)) * width, width, axis=1)
        for i in range(2) for j in range(2)
    ]
    cot = sum(
        jnp.einsum("btf,cf->btc", grad, part, preferred_element_type=jnp.float32)
        for grad, part in zip((grad_out, near, far, cross), blocks)
    ).astype(jnp.bfloat16)
    split = split_slots("split_values", z, (values, values_tan, cot))
    plane, split = lax.optimization_barrier((plane, split))
    plane_v = to_plane(split)

    packed = repack(functools.partial(keys_kernel, heads), "pack_keys", z, plane, [(chips, rows + window, 2 * HD)])[0]
    recv_k = over_chips(packed)
    recv_k, plane_v = lax.optimization_barrier((recv_k, plane_v))
    other_k = swap(recv_k, "c")
    packed = repack(functools.partial(values_pack_kernel, heads), "pack_values", z, plane_v, [(chips, 2 * rows + window, HD)])[0]
    recv_v = over_chips(packed)

    probs, weights = attention_weights(z, recv_k, other_k, rows, window)
    recv_v, probs, weights = lax.optimization_barrier((recv_v, probs, weights))
    other_v = swap(recv_v, "c")
    out, dsum = attention_values(z, recv_v, other_v, probs, weights, rows, window)
    back = over_chips(out)
    dq, own_grads, other_grads = attention_grads(z, recv_k, other_k, recv_v, other_v, probs, dsum, rows, window)
    back, dq, own_grads, other_grads = lax.optimization_barrier((back, dq, own_grads, other_grads))
    got = swap(other_grads, "c")
    merged = repack(merge_kernel, "merge", z, [own_grads, got, dq], [(chips, 2 * rows + window, HD)])[0]
    back, merged = lax.optimization_barrier((back, merged))

    shapes = [(tokens // 2, 2 * features)] * slots
    home = from_plane(repack(functools.partial(out_unpack_kernel, heads), "unpack_out", z, [back], shapes))
    grads = over_chips(merged)
    home, grads = lax.optimization_barrier((home, grads))
    attn, attn_tan = join_slots("join_out", z, home, 2, clips)
    both = jnp.concatenate([attn, attn_tan], axis=0).reshape(2 * clips * tokens, features)

    def project(part):
        return jnp.dot(both, part, preferred_element_type=jnp.float32)

    give = swap(jnp.concatenate([project(w_near), project(w_cross)], axis=1).astype(jnp.bfloat16), "c")
    give = give.astype(jnp.float32)
    got = swap((project(w_far) + give[:, width:]).astype(jnp.bfloat16), "w")
    outs = (project(w_own) + give[:, :width] + got.astype(jnp.float32)).astype(jnp.bfloat16)
    outs = outs.reshape(2, clips, tokens, -1)

    shapes = [(tokens // 2, 3 * features)] * slots
    home = from_plane(repack(functools.partial(grads_unpack_kernel, heads), "unpack_grads", z, [grads], shapes))
    grad_k, grad_v, grad_q = join_slots("join_grads", z, home, 3, clips)
    return outs[0], outs[1], grad_q, grad_k, grad_v


def solution(mesh):
    seq, tp = ("x", "y", "z"), ("w", "c")
    fine = Mesh(mesh.devices.reshape(4, 4, 4, 2, 2), seq + tp)
    split = P(None, seq, tp)
    return jax.shard_map(
        local,
        mesh=fine,
        in_specs=(split,) * 6 + (P(tp, None), split),
        out_specs=(split,) * 5,
        check_vma=False,
    )
```

```python
import functools

import jax
import jax.numpy as jnp
from jax import lax
from jax.experimental import pallas as pl
from jax.experimental.pallas import tpu as pltpu
from jax.sharding import Mesh, PartitionSpec as P

HD = 128
SCALE = HD ** (-0.5)
LOG2E = 1.4426950408889634
SUB = 16
W_GROUP, W_UNROLL = 4, 4
V_GROUP, V_UNROLL = 8, True
G_GROUP, G_UNROLL = 8, True
VMEM_LIMIT = 52 * 2**20
NT = (((1,), (1,)), ((), ()))
NN = (((1,), (0,)), ((), ()))


def dot(a, b, dims=NN):
    return lax.dot_general(a, b, dims, preferred_element_type=jnp.float32)


def piece(ref, j, group, first, count, lanes=slice(None)):
    block = ref[pl.ds(j * group, group), first:first + count, lanes]
    return block.reshape(group * count, block.shape[-1])


def key_rows(half, j, group, blocks, rows):
    start = (half * blocks + j * group) * rows
    return pl.ds(pl.multiple_of(start, group * rows), group * rows)


def weights_kernel(rows, z_ref, q_ref, ka_ref, kb_ref, p_ref, w_ref, s_scr, t_scr):
    blocks = ka_ref.shape[0]
    tile = p_ref.shape[1]
    qtq = q_ref[...].reshape(tile, 2 * HD)
    q = qtq[:, HD:]

    top = jnp.full((1, tile), -jnp.inf, jnp.float32)
    for half, ref in enumerate((ka_ref, kb_ref)):
        def scores(j, top, half=half, ref=ref):
            here = key_rows(half, j, W_GROUP, blocks, rows)
            both = piece(ref, j, W_GROUP, 0, rows)
            s = dot(both[:, :HD], q, NT)
            s_scr[here, :] = s
            t_scr[here, :] = dot(both, qtq, NT)
            return jnp.maximum(top, jnp.max(s, axis=0, keepdims=True))
        top = lax.fori_loop(0, blocks // W_GROUP, scores, top, unroll=W_UNROLL)

    zero = jnp.zeros((1, tile), jnp.float32)

    def sums(j, carry):
        total, slope = carry
        here = key_rows(0, j, W_GROUP, blocks, rows)
        e = jnp.exp2((s_scr[here, :] - top) * (SCALE * LOG2E))
        s_scr[here, :] = e
        total += jnp.sum(e, axis=0, keepdims=True)
        slope += jnp.sum(e * t_scr[here, :], axis=0, keepdims=True)
        return total, slope

    total, slope = lax.fori_loop(0, 2 * blocks // W_GROUP, sums, (zero, zero), unroll=W_UNROLL)
    inv = 1.0 / total
    slope = slope * inv

    def store(j, carry):
        here = key_rows(0, j, W_GROUP, blocks, rows)
        p = s_scr[here, :] * inv
        p_ref[here, :] = p.astype(jnp.bfloat16)
        w_ref[here, :] = (p * (t_scr[here, :] - slope)).astype(jnp.bfloat16)
        return carry

    lax.fori_loop(0, 2 * blocks // W_GROUP, store, 0, unroll=W_UNROLL)


def values_kernel(rows, z_ref, g_ref, va_ref, vb_ref, p_ref, w_ref, out_ref, d_ref, vt_scr):
    blocks = va_ref.shape[0]
    tile = p_ref.shape[1]

    @pl.when(pl.program_id(0) == 0)
    def _():
        for half, ref in enumerate((va_ref, vb_ref)):
            def turn(j, carry, half=half, ref=ref):
                here = key_rows(half, j, V_GROUP, blocks, rows)
                vt_scr[0:HD, here] = piece(ref, j, V_GROUP, 0, rows).T
                vt_scr[HD:, here] = piece(ref, j, V_GROUP, rows, rows).T
                return carry
            lax.fori_loop(0, blocks // V_GROUP, turn, 0, unroll=V_UNROLL)

    def add(j, carry):
        both, tan = carry
        here = key_rows(0, j, V_GROUP, blocks, rows)
        both += dot(vt_scr[:, here], p_ref[here, :])
        tan += dot(vt_scr[0:HD, here], w_ref[here, :])
        return both, tan

    zeros = jnp.zeros((2 * HD, tile), jnp.float32), jnp.zeros((HD, tile), jnp.float32)
    both, tan = lax.fori_loop(0, 2 * blocks // V_GROUP, add, zeros, unroll=V_UNROLL)
    attn = both[0:HD].astype(jnp.bfloat16)
    g = g_ref[...].reshape(tile, HD)
    d_ref[...] = jnp.sum(attn.astype(jnp.float32) * g.astype(jnp.float32).T, axis=0, keepdims=True)
    out_ref[:, :, 0:HD] = both[0:HD].T.astype(jnp.bfloat16).reshape(-1, SUB, HD)
    out_ref[:, :, HD:] = (both[HD:] + SCALE * tan).T.astype(jnp.bfloat16).reshape(-1, SUB, HD)


def grads_kernel(rows, z_ref, q_ref, g_ref, ka_ref, kb_ref, va_ref, vb_ref, p_ref, d_ref, dq_ref, oa_ref, ob_ref, kt_scr, k_scr, v_scr):
    blocks = ka_ref.shape[0]
    tile = p_ref.shape[1]
    step = pl.program_id(0)
    q = q_ref[...].reshape(tile, 2 * HD)[:, HD:]
    g = g_ref[...].reshape(tile, HD)
    dsum = d_ref[...]

    @pl.when(step == 0)
    def _():
        for half, ref in enumerate((ka_ref, kb_ref)):
            def turn(j, carry, half=half, ref=ref):
                kt_scr[:, key_rows(half, j, G_GROUP, blocks, rows)] = piece(ref, j, G_GROUP, 0, rows, slice(0, HD)).T
                return carry
            lax.fori_loop(0, blocks // G_GROUP, turn, 0, unroll=G_UNROLL)
        k_scr[...] = jnp.zeros_like(k_scr)
        v_scr[...] = jnp.zeros_like(v_scr)

    dq = jnp.zeros((HD, tile), jnp.float32)
    for half, ref in enumerate((va_ref, vb_ref)):
        def add(j, dq, half=half, ref=ref):
            here = key_rows(half, j, G_GROUP, blocks, rows)
            p = p_ref[here, :]
            slopes = dot(piece(ref, j, G_GROUP, 0, rows), g, NT) - dsum
            ds = (p.astype(jnp.float32) * slopes).astype(jnp.bfloat16)
            k_scr[here, :] += dot(ds, q)
            v_scr[here, :] += dot(p, g)
            return dq + dot(kt_scr[:, here], ds)
        dq = lax.fori_loop(0, blocks // G_GROUP, add, dq, unroll=G_UNROLL)
    dq_ref[...] = (SCALE * dq).T.astype(jnp.bfloat16).reshape(-1, SUB, HD)

    @pl.when(step == pl.num_programs(0) - 1)
    def _():
        for half, ref in enumerate((oa_ref, ob_ref)):
            def give(j, carry, half=half, ref=ref):
                here = key_rows(half, j, G_GROUP, blocks, rows)
                group = pl.ds(j * G_GROUP, G_GROUP)
                ref[group, 0:rows, :] = (SCALE * k_scr[here, :]).astype(jnp.bfloat16).reshape(G_GROUP, rows, HD)
                ref[group, rows:, :] = v_scr[here, :].astype(jnp.bfloat16).reshape(G_GROUP, rows, HD)
                return carry
            lax.fori_loop(0, blocks // G_GROUP, give, 0, unroll=G_UNROLL)


def whole(array):
    return pl.BlockSpec(array.shape, lambda i, s: (0,) * len(array.shape))


def kernel_call(body, name, grid, scalars, ins, outs, scratch, flops=0, bytes_accessed=4 * 2**20, limit=VMEM_LIMIT):
    arrays, in_specs = zip(*ins)
    shapes, out_specs = zip(*outs)
    return pl.pallas_call(
        body,
        grid_spec=pltpu.PrefetchScalarGridSpec(
            num_scalar_prefetch=1,
            grid=(grid,),
            in_specs=list(in_specs),
            out_specs=list(out_specs),
            scratch_shapes=scratch,
        ),
        out_shape=list(shapes),
        name=name,
        compiler_params=pltpu.CompilerParams(vmem_limit_bytes=limit),
        cost_estimate=pl.CostEstimate(flops=flops, bytes_accessed=bytes_accessed, transcendentals=0),
    )(scalars, *arrays)


def specs(blocks, rows, window):
    tile = blocks * SUB
    keys = 2 * blocks * rows
    q_spec = pl.BlockSpec((blocks, SUB, 2 * HD), lambda i, s: (0, rows // SUB + i, 0))
    g_spec = pl.BlockSpec((blocks, SUB, HD), lambda i, s: (0, 2 * rows // SUB + i, 0))
    p_spec = pl.BlockSpec((keys, tile), lambda i, s: (0, i))
    d_spec = pl.BlockSpec((1, tile), lambda i, s: (0, i))
    return q_spec, g_spec, p_spec, d_spec, keys, tile, window // SUB


def attention_weights(z, recv_k, other_k, rows, window):
    q_spec, _, p_spec, _, keys, tile, grid = specs(recv_k.shape[0], rows, window)
    p_shape = jax.ShapeDtypeStruct((keys, grid * tile), jnp.bfloat16)
    return kernel_call(
        functools.partial(weights_kernel, rows), "weights", grid, z,
        [(recv_k, q_spec), (recv_k, whole(recv_k)), (other_k, whole(other_k))],
        [(p_shape, p_spec), (p_shape, p_spec)],
        [pltpu.VMEM((keys, tile), jnp.float32), pltpu.VMEM((keys, tile), jnp.float32)],
        8 * keys * grid * tile * HD, 32 * 2**20)


def attention_values(z, recv_v, other_v, probs, weights, rows, window):
    blocks = recv_v.shape[0]
    _, g_spec, p_spec, d_spec, keys, tile, grid = specs(blocks, rows, window)
    out_shape = jax.ShapeDtypeStruct((blocks, window, 2 * HD), jnp.bfloat16)
    d_shape = jax.ShapeDtypeStruct((1, grid * tile), jnp.float32)
    return kernel_call(
        functools.partial(values_kernel, rows), "values", grid, z,
        [(recv_v, g_spec), (recv_v, whole(recv_v)), (other_v, whole(other_v)), (probs, p_spec), (weights, p_spec)],
        [(out_shape, pl.BlockSpec((blocks, SUB, 2 * HD), lambda i, s: (0, i, 0))), (d_shape, d_spec)],
        [pltpu.VMEM((2 * HD, keys), jnp.bfloat16)],
        6 * keys * grid * tile * HD, 16 * 2**20)


def attention_grads(z, recv_k, other_k, recv_v, other_v, probs, dsum, rows, window):
    blocks = recv_v.shape[0]
    q_spec, g_spec, p_spec, d_spec, keys, tile, grid = specs(blocks, rows, window)
    dq_shape = jax.ShapeDtypeStruct((blocks, window, HD), jnp.bfloat16)
    shape = jax.ShapeDtypeStruct((blocks, 2 * rows, HD), jnp.bfloat16)
    return kernel_call(
        functools.partial(grads_kernel, rows), "grads", grid, z,
        [(recv_k, q_spec), (recv_v, g_spec), (recv_k, whole(recv_k)), (other_k, whole(other_k)),
         (recv_v, whole(recv_v)), (other_v, whole(other_v)), (probs, p_spec), (dsum, d_spec)],
        [(dq_shape, pl.BlockSpec((blocks, SUB, HD), lambda i, s: (0, i, 0))),
         (shape, whole(shape)), (shape, whole(shape))],
        [pltpu.VMEM((HD, keys), jnp.bfloat16), pltpu.VMEM((keys, HD), jnp.float32), pltpu.VMEM((keys, HD), jnp.float32)],
        10 * keys * grid * tile * HD, 32 * 2**20)


THIRDS = 3
SWAP = [(0, 1), (1, 0)]


def swap(array, axis):
    return lax.ppermute(array, axis, SWAP)


def along_z(pieces):
    count = len(pieces)
    routes = [[(i, (i + k) % count) for i in range(count)] for k in range(count)]
    return [pieces[0]] + [lax.ppermute(a, "z", route) for a, route in zip(pieces[1:], routes[1:])]


def over_chips(array):
    return lax.all_to_all(array, ("x", "y"), 0, 0, tiled=True)


def plane_at(place_ref, shift, count):
    return lax.rem(place_ref[0] + shift + count, count)


def split_kernel(place_ref, *refs):
    count = 4
    ins, outs = refs[:-count], refs[-count:]
    kinds = len(ins) // 2
    clips, tokens, width = ins[0].shape
    rows = tokens // 2
    core = place_ref[1]
    start = pl.multiple_of(core * rows, rows)
    for k, out in enumerate(outs):
        slot = plane_at(place_ref, k, count)
        part, clip = slot // clips, lax.rem(slot, clips)

        for mine, group in ((True, ins[:kinds]), (False, ins[kinds:])):
            @pl.when((part == core) == mine)
            def _(out=out, group=group, clip=clip):
                for index, ref in enumerate(group):
                    out[:, index * width:(index + 1) * width] = ref[clip, pl.ds(start, rows), :]


def keep_kernel(c_ref, *refs):
    out = refs[-1]
    kinds = len(refs) // 2
    clips, tokens, width = refs[0].shape
    rows = tokens // 2
    core = c_ref[0]
    start = pl.multiple_of(core * rows, rows)
    for part, group in ((core, refs[:kinds]), (1 - core, refs[kinds:2 * kinds])):
        for clip in range(clips):
            for index, ref in enumerate(group):
                out[part * clips + clip, :, index * width:(index + 1) * width] = ref[clip, pl.ds(start, rows), :]


def home_kernel(c_ref, back_ref, got_ref, *outs):
    clips, tokens, width = outs[0].shape
    rows = tokens // 2
    core = c_ref[0]
    for clip in range(clips):
        for index, out in enumerate(outs):
            lanes = slice(index * width, (index + 1) * width)
            out[clip, pl.ds(pl.multiple_of(core * rows, rows), rows), :] = back_ref[core * clips + clip, :, lanes]
            out[clip, pl.ds(pl.multiple_of((1 - core) * rows, rows), rows), :] = got_ref[core * clips + clip, :, lanes]


def keys_kernel(heads, z_ref, *refs):
    plane_ref, out = refs
    rows = plane_ref.shape[0]
    window = out.shape[1] - rows
    width = heads * HD
    for head in range(heads):
        for kind in range(4):
            source = slice(kind * width + head * HD, kind * width + (head + 1) * HD)
            lanes = slice((kind % 2) * HD, (kind % 2 + 1) * HD)
            whole_block = plane_ref[:, source]
            for third in range(THIRDS):
                chip = head * THIRDS + third
                if kind < 2:
                    out[chip, 0:rows, lanes] = whole_block
                else:
                    first = third * window
                    count = min(window, rows - first)
                    out[chip, rows:rows + count, lanes] = whole_block[first:first + count]
                    if count < window:
                        out[chip, rows + count:, lanes] = jnp.zeros((window - count, HD), out.dtype)
    for chip in range(heads * THIRDS, out.shape[0]):
        out[chip] = jnp.zeros(out.shape[1:], out.dtype)


def values_pack_kernel(heads, place_ref, *refs):
    ins, out, scr = refs[:-2], refs[-2], refs[-1]
    part = ins[0].shape[0]
    rows = part * len(ins)
    for k, ref in enumerate(ins):
        scr[pl.ds(pl.multiple_of(plane_at(place_ref, -k, len(ins)) * part, part), part), :] = ref[...]
    window = out.shape[1] - 2 * rows
    width = heads * HD
    for head in range(heads):
        for kind in range(3):
            source = slice(kind * width + head * HD, kind * width + (head + 1) * HD)
            whole_block = scr[:, source]
            for third in range(THIRDS):
                chip = head * THIRDS + third
                if kind < 2:
                    out[chip, kind * rows:(kind + 1) * rows, :] = whole_block
                else:
                    first = third * window
                    count = min(window, rows - first)
                    out[chip, 2 * rows:2 * rows + count, :] = whole_block[first:first + count]
                    if count < window:
                        out[chip, 2 * rows + count:, :] = jnp.zeros((window - count, HD), out.dtype)
    for chip in range(heads * THIRDS, out.shape[0]):
        out[chip] = jnp.zeros(out.shape[1:], out.dtype)


def out_unpack_kernel(heads, place_ref, back_ref, *refs):
    outs, scr = refs[:-1], refs[-1]
    part = outs[0].shape[0]
    window = back_ref.shape[1]
    rows = part * len(outs)
    width = heads * HD
    for head in range(heads):
        for kind in range(2):
            lanes = slice(kind * HD, (kind + 1) * HD)
            pieces = [
                back_ref[head * THIRDS + third, 0:min(window, rows - third * window), lanes]
                for third in range(THIRDS)
            ]
            scr[:, kind * width + head * HD:kind * width + (head + 1) * HD] = jnp.concatenate(pieces, axis=0)
    for k, out in enumerate(outs):
        out[...] = scr[pl.ds(pl.multiple_of(plane_at(place_ref, k, len(outs)) * part, part), part), :]


def join_out_kernel(place_ref, *refs):
    ins, own_ref, other_ref = refs[:-2], refs[-2], refs[-1]
    rows, width = ins[0].shape
    clips, width = len(ins) // 2, width // 2
    for k, ref in enumerate(ins):
        slot = plane_at(place_ref, -k, len(ins))
        part, clip = slot // clips, lax.rem(slot, clips)
        for mine, out in ((True, own_ref), (False, other_ref)):
            @pl.when((part == place_ref[1]) == mine)
            def _(ref=ref, out=out, clip=clip):
                for kind in range(2):
                    first = pl.multiple_of((kind * clips + clip) * rows, rows)
                    out[pl.ds(first, rows), :] = ref[:, kind * width:(kind + 1) * width]


def home_out_kernel(c_ref, keep_ref, got_ref, *outs):
    clips, tokens, width = outs[0].shape
    rows = tokens // 2
    core = c_ref[0]
    for ref, half in ((keep_ref, core), (got_ref, 1 - core)):
        for kind, out in enumerate(outs):
            for clip in range(clips):
                first = (kind * clips + clip) * rows
                lanes = pl.ds(pl.multiple_of(core * width, HD), width)
                out[clip, pl.ds(pl.multiple_of(half * rows, rows), rows), :] = ref[first:first + rows, lanes]


def grads_unpack_kernel(heads, z_ref, back_ref, out_ref):
    part = out_ref.shape[1]
    rows = part * out_ref.shape[0]
    window = back_ref.shape[1] - 2 * rows
    width = heads * HD
    for head in range(heads):
        for kind in range(3):
            chips = [head * THIRDS + third for third in range(THIRDS)]
            if kind < 2:
                column = sum(
                    back_ref[chip, kind * rows:(kind + 1) * rows, :].astype(jnp.float32) for chip in chips
                ).astype(jnp.bfloat16)
            else:
                column = jnp.concatenate([
                    back_ref[chip, 2 * rows:2 * rows + min(window, rows - third * window), :]
                    for third, chip in enumerate(chips)
                ], axis=0)
            for d in range(out_ref.shape[0]):
                lanes = slice(kind * width + head * HD, kind * width + (head + 1) * HD)
                out_ref[d, :, lanes] = column[d * part:(d + 1) * part]


def merge_kernel(z_ref, own_ref, got_ref, dq_ref, out_ref):
    rows = got_ref.shape[1]
    total = own_ref[...].astype(jnp.float32) + got_ref[...].astype(jnp.float32)
    out_ref[:, 0:rows, :] = total.astype(jnp.bfloat16)
    out_ref[:, rows:, :] = dq_ref[...]


def repack(body, name, z, ins, shapes, scratch=(), limit=VMEM_LIMIT):
    shapes = [jax.ShapeDtypeStruct(s, jnp.bfloat16) for s in shapes]
    return kernel_call(body, name, 1, z, [(a, whole(a)) for a in ins], [(s, whole(s)) for s in shapes], list(scratch), limit=limit)


def over_planes(array):
    return lax.all_to_all(array, "z", 0, 0, tiled=True)


def local(queries, keys, values, queries_tan, keys_tan, values_tan, w_out, grad_out):
    w, c = lax.axis_index("w"), lax.axis_index("c")
    z = lax.axis_index("z").astype(jnp.int32).reshape(1)
    core = c.astype(jnp.int32).reshape(1)
    place = jnp.concatenate([z, core])
    clips, tokens, features = queries.shape
    heads = features // HD
    chips = lax.axis_size(("x", "y"))
    slots = 2 * clips
    rows = slots * tokens // 2
    window = pl.cdiv(pl.cdiv(rows, THIRDS), SUB) * SUB

    w_other = swap(w_out, "c")

    far = swap(grad_out, "w")
    near = swap(grad_out, "c")
    kinds = (keys, keys_tan, queries_tan, queries)
    got = tuple(swap(kind, "c") for kind in kinds)
    got_values = tuple(swap(kind, "c") for kind in (values, values_tan))
    kept = repack(keep_kernel, "keep_keys", core, kinds + got, [(slots, tokens // 2, len(kinds) * features)],
                  limit=60 * 2**20)[0]
    kept, far = lax.optimization_barrier((kept, far))
    plane = over_planes(kept).reshape(rows, -1)
    cross = swap(far, "c")
    width = grad_out.shape[2]
    blocks = [
        lax.dynamic_slice_in_dim(w_out, ((w ^ i) * 2 + (c ^ j)) * width, width, axis=1)
        for i in range(2) for j in range(2)
    ]
    cot = sum(
        jnp.einsum("btf,cf->btc", grad, part, preferred_element_type=jnp.float32)
        for grad, part in zip((grad_out, near, far, cross), blocks)
    ).astype(jnp.bfloat16)
    kinds = (values, values_tan, cot)
    got = got_values + (swap(cot, "c"),)
    shape = (tokens // 2, len(kinds) * features)
    split = repack(split_kernel, "split_values", place, kinds + got, [shape] * slots)
    plane, split = lax.optimization_barrier((plane, split))
    plane_v = along_z(split)

    packed = repack(functools.partial(keys_kernel, heads), "pack_keys", z, [plane], [(chips, rows + window, 2 * HD)])[0]
    recv_k = over_chips(packed)
    recv_k, plane_v = lax.optimization_barrier((recv_k, plane_v))
    other_k = swap(recv_k, "c")
    packed = repack(functools.partial(values_pack_kernel, heads), "pack_values", place, plane_v, [(chips, 2 * rows + window, HD)],
                    [pltpu.VMEM((rows, 3 * features), jnp.bfloat16)])[0]
    recv_v = over_chips(packed)

    probs, weights = attention_weights(z, recv_k, other_k, rows, window)
    recv_v, probs, weights = lax.optimization_barrier((recv_v, probs, weights))
    other_v = swap(recv_v, "c")
    out, dsum = attention_values(z, recv_v, other_v, probs, weights, rows, window)
    back = over_chips(out)
    dq, own_grads, other_grads = attention_grads(z, recv_k, other_k, recv_v, other_v, probs, dsum, rows, window)
    back, dq, own_grads, other_grads = lax.optimization_barrier((back, dq, own_grads, other_grads))
    got = swap(other_grads, "c")
    merged = repack(merge_kernel, "merge", z, [own_grads, got, dq], [(chips, 2 * rows + window, HD)])[0]
    back, merged = lax.optimization_barrier((back, merged))
    grads = over_chips(merged)

    shape = (tokens // 2, 2 * features)
    home = along_z(repack(functools.partial(out_unpack_kernel, heads), "unpack_out", place, [back], [shape] * slots,
                          [pltpu.VMEM((rows, 2 * features), jnp.bfloat16)]))
    home, grads = lax.optimization_barrier((home, grads))
    own, other = repack(join_out_kernel, "join_out", place, home, [(slots * tokens // 2, features)] * 2)

    def project(chip):
        parts = [
            jnp.dot(rows_of, lax.dynamic_slice_in_dim(weight, chip * 2 * width, 2 * width, axis=1),
                    preferred_element_type=jnp.float32)
            for rows_of, weight in ((own, w_out), (other, w_other))
        ]
        return parts[0] + parts[1]

    got = swap(project(1 - w).astype(jnp.bfloat16), "w")
    total = (project(w) + got.astype(jnp.float32)).astype(jnp.bfloat16)
    outs = repack(home_out_kernel, "home_out", core, [total, swap(total, "c")], [(clips, tokens, width)] * 2)

    shape = (slots, tokens // 2, 3 * features)
    back = over_planes(repack(functools.partial(grads_unpack_kernel, heads), "unpack_grads", z, [grads], [shape])[0])
    grad_k, grad_v, grad_q = repack(home_kernel, "home_grads", core, [back, swap(back, "c")], [queries.shape] * 3)
    return outs[0], outs[1], grad_q, grad_k, grad_v


def solution(mesh):
    seq, tp = ("x", "y", "z"), ("w", "c")
    fine = Mesh(mesh.devices.reshape(4, 4, 4, 2, 2), seq + tp)
    split = P(None, seq, tp)
    return jax.shard_map(
        local,
        mesh=fine,
        in_specs=(split,) * 6 + (P(tp, None), split),
        out_specs=(split,) * 5,
        check_vma=False,
    )
```

```python
import functools

import jax
import jax.numpy as jnp
from jax import lax
from jax.experimental import pallas as pl
from jax.experimental.pallas import tpu as pltpu
from jax.sharding import Mesh, PartitionSpec as P

HD = 128
SCALE = HD ** (-0.5)
LOG2E = 1.4426950408889634
SUB = 16
W_GROUP, W_UNROLL = 4, 4
V_GROUP = 8
G_GROUP = 8
VMEM_LIMIT = 52 * 2**20
NT = (((1,), (1,)), ((), ()))
NN = (((1,), (0,)), ((), ()))


def dot(a, b, dims=NN):
    return lax.dot_general(a, b, dims, preferred_element_type=jnp.float32)


def piece(ref, j, group, first, count, lanes=slice(None)):
    block = ref[pl.ds(j * group, group), first:first + count, lanes]
    return block.reshape(group * count, block.shape[-1])


def key_rows(half, j, group, blocks, rows):
    start = (half * blocks + j * group) * rows
    return pl.ds(pl.multiple_of(start, group * rows), group * rows)


def weights_kernel(rows, z_ref, q_ref, ka_ref, kb_ref, p_ref, w_ref, s_scr, t_scr):
    blocks = ka_ref.shape[0]
    tile = p_ref.shape[1]
    qtq = q_ref[...].reshape(tile, 2 * HD)
    q = qtq[:, HD:]

    top = jnp.full((1, tile), -jnp.inf, jnp.float32)
    for half, ref in enumerate((ka_ref, kb_ref)):
        def scores(j, top, half=half, ref=ref):
            here = key_rows(half, j, W_GROUP, blocks, rows)
            both = piece(ref, j, W_GROUP, 0, rows)
            s = dot(both[:, :HD], q, NT)
            s_scr[here, :] = s
            t_scr[here, :] = dot(both, qtq, NT)
            return jnp.maximum(top, jnp.max(s, axis=0, keepdims=True))
        top = lax.fori_loop(0, blocks // W_GROUP, scores, top, unroll=W_UNROLL)

    zero = jnp.zeros((1, tile), jnp.float32)

    def sums(j, carry):
        total, slope = carry
        here = key_rows(0, j, W_GROUP, blocks, rows)
        e = jnp.exp2((s_scr[here, :] - top) * (SCALE * LOG2E))
        s_scr[here, :] = e
        total += jnp.sum(e, axis=0, keepdims=True)
        slope += jnp.sum(e * t_scr[here, :], axis=0, keepdims=True)
        return total, slope

    total, slope = lax.fori_loop(0, 2 * blocks // W_GROUP, sums, (zero, zero), unroll=W_UNROLL)
    inv = 1.0 / total
    slope = slope * inv

    def store(j, carry):
        here = key_rows(0, j, W_GROUP, blocks, rows)
        p = s_scr[here, :] * inv
        p_ref[here, :] = p.astype(jnp.bfloat16)
        w_ref[here, :] = (p * (t_scr[here, :] - slope)).astype(jnp.bfloat16)
        return carry

    lax.fori_loop(0, 2 * blocks // W_GROUP, store, 0, unroll=W_UNROLL)


def window_rows(refs):
    return jnp.concatenate([ref[...].reshape(-1, HD) for ref in refs], axis=0)


def put_rows(ref, lanes, value):
    blocks, window, _ = ref.shape
    tile = blocks * SUB
    for i in range(window // SUB):
        ref[:, i * SUB:(i + 1) * SUB, lanes] = value[i * tile:(i + 1) * tile].astype(ref.dtype).reshape(blocks, SUB, HD)


def values_kernel(last, z_ref, v_ref, t_ref, p_ref, w_ref, *refs):
    step = pl.program_id(0)
    if last:
        *g_refs, start_ref, out_ref, d_ref, acc = refs
    else:
        acc = refs[0]
    chunk = p_ref.shape[0]
    v = v_ref[...].reshape(chunk, HD)
    both = jnp.concatenate([v, t_ref[...].reshape(chunk, HD)], axis=1).T

    @pl.when(step == 0)
    def _():
        acc[...] = start_ref[...] if last else jnp.zeros_like(acc)

    acc[0:2 * HD, :] += dot(both, p_ref[...])
    acc[2 * HD:, :] += dot(both[0:HD], w_ref[...])

    if last:
        @pl.when(step == pl.num_programs(0) - 1)
        def _():
            g = window_rows(g_refs).astype(jnp.float32)
            attn = acc[0:HD, :].T.astype(jnp.bfloat16)
            dsum = jnp.sum(attn.astype(jnp.float32) * g, axis=1, keepdims=True)
            d_ref[...] = jnp.broadcast_to(dsum, (dsum.shape[0], HD)).T[0:1, :]
            tan = acc[HD:2 * HD, :] + SCALE * acc[2 * HD:, :]
            put_rows(out_ref, slice(0, HD), attn)
            put_rows(out_ref, slice(HD, 2 * HD), tan.T)


def grads_kernel(last, z_ref, k_ref, v_ref, p_ref, d_ref, *refs):
    step = pl.program_id(0)
    chunk, queries = p_ref.shape
    count = (len(refs) - (5 if last else 3)) // 2
    q, g, refs = window_rows(refs[:count]), window_rows(refs[count:2 * count]), refs[2 * count:]
    if last:
        start_ref, dk_ref, dv_ref, dq_ref, acc = refs
    else:
        dk_ref, dv_ref, acc = refs
    k = k_ref[...].reshape(chunk, HD)
    v = v_ref[...].reshape(chunk, HD)
    p = p_ref[...]

    @pl.when(step == 0)
    def _():
        acc[...] = start_ref[...] if last else jnp.zeros_like(acc)

    ds = (p.astype(jnp.float32) * (dot(v, g, NT) - d_ref[...])).astype(jnp.bfloat16)
    dk_ref[...] = (SCALE * dot(ds, q)).astype(jnp.bfloat16).reshape(dk_ref.shape)
    dv_ref[...] = dot(p, g).astype(jnp.bfloat16).reshape(dv_ref.shape)
    acc[...] += dot(k.T, ds)

    if last:
        @pl.when(step == pl.num_programs(0) - 1)
        def _():
            put_rows(dq_ref, slice(0, HD), (SCALE * acc[...]).T)


def whole(array):
    return pl.BlockSpec(array.shape, lambda i, s: (0,) * len(array.shape))


def kernel_call(body, name, grid, scalars, ins, outs, scratch, flops=0, bytes_accessed=4 * 2**20, limit=VMEM_LIMIT):
    arrays, in_specs = zip(*ins)
    shapes, out_specs = zip(*outs)
    return pl.pallas_call(
        body,
        grid_spec=pltpu.PrefetchScalarGridSpec(
            num_scalar_prefetch=1,
            grid=(grid,),
            in_specs=list(in_specs),
            out_specs=list(out_specs),
            scratch_shapes=scratch,
        ),
        out_shape=list(shapes),
        name=name,
        compiler_params=pltpu.CompilerParams(vmem_limit_bytes=limit),
        cost_estimate=pl.CostEstimate(flops=flops, bytes_accessed=bytes_accessed, transcendentals=0),
    )(scalars, *arrays)


def specs(blocks, rows, window):
    tile = blocks * SUB
    keys = 2 * blocks * rows
    q_spec = pl.BlockSpec((blocks, SUB, 2 * HD), lambda i, s: (0, rows // SUB + i, 0))
    g_spec = pl.BlockSpec((blocks, SUB, HD), lambda i, s: (0, 2 * rows // SUB + i, 0))
    p_spec = pl.BlockSpec((keys, tile), lambda i, s: (0, i))
    d_spec = pl.BlockSpec((1, tile), lambda i, s: (0, i))
    return q_spec, g_spec, p_spec, d_spec, keys, tile, window // SUB


def attention_weights(z, recv_k, other_k, rows, window):
    q_spec, _, p_spec, _, keys, tile, grid = specs(recv_k.shape[0], rows, window)
    p_shape = jax.ShapeDtypeStruct((keys, grid * tile), jnp.bfloat16)
    return kernel_call(
        functools.partial(weights_kernel, rows), "weights", grid, z,
        [(recv_k, q_spec), (recv_k, whole(recv_k)), (other_k, whole(other_k))],
        [(p_shape, p_spec), (p_shape, p_spec)],
        [pltpu.VMEM((keys, tile), jnp.float32), pltpu.VMEM((keys, tile), jnp.float32)],
        8 * keys * grid * tile * HD, 32 * 2**20)


def windows(array, first, window, lane):
    blocks = array.shape[0]
    return [
        (array, pl.BlockSpec((blocks, SUB, HD), lambda i, s, at=first // SUB + part: (0, at, lane)))
        for part in range(window // SUB)
    ]


def attention_values(z, recv_v, other_v, probs, weights, rows, window):
    blocks = recv_v.shape[0]
    keys, queries = probs.shape
    half = blocks // V_GROUP
    sums = jax.ShapeDtypeStruct((3 * HD, queries), jnp.float32)
    out_shape = jax.ShapeDtypeStruct((blocks, window, 2 * HD), jnp.bfloat16)
    d_shape = jax.ShapeDtypeStruct((1, queries), jnp.float32)

    def ins(array, first):
        p_spec = pl.BlockSpec((V_GROUP * rows, queries), lambda i, s: (first + i, 0))
        return [
            (array, pl.BlockSpec((V_GROUP, rows, HD), lambda i, s: (i, 0, 0))),
            (array, pl.BlockSpec((V_GROUP, rows, HD), lambda i, s: (i, 1, 0))),
            (probs, p_spec), (weights, p_spec),
        ]

    start = kernel_call(
        functools.partial(values_kernel, False), "values_own", half, z, ins(recv_v, 0),
        [(sums, whole(sums))], [], 3 * keys * queries * HD, 8 * 2**20)[0]
    g = windows(recv_v, 2 * rows, window, 0)
    return kernel_call(
        functools.partial(values_kernel, True), "values_other", half, z,
        ins(other_v, half) + g + [(start, whole(start))],
        [(out_shape, whole(out_shape)), (d_shape, whole(d_shape))],
        [pltpu.VMEM(sums.shape, sums.dtype)], 3 * keys * queries * HD, 8 * 2**20)


def attention_grads(z, recv_k, other_k, recv_v, other_v, probs, dsum, rows, window):
    blocks = recv_v.shape[0]
    keys, queries = probs.shape
    half = blocks // G_GROUP
    dq_shape = jax.ShapeDtypeStruct((blocks, window, HD), jnp.bfloat16)
    shape = jax.ShapeDtypeStruct((blocks, rows, HD), jnp.bfloat16)
    sums = jax.ShapeDtypeStruct((HD, queries), jnp.float32)
    g = windows(recv_v, 2 * rows, window, 0)
    q = windows(recv_k, rows, window, 1)

    def ins(k, v, first):
        block = pl.BlockSpec((G_GROUP, rows, HD), lambda i, s: (i, 0, 0))
        return [
            (k, block), (v, block),
            (probs, pl.BlockSpec((G_GROUP * rows, queries), lambda i, s: (first + i, 0))),
            (dsum, whole(dsum)),
        ] + q + g

    out = (shape, pl.BlockSpec((G_GROUP, rows, HD), lambda i, s: (i, 0, 0)))
    other_dk, other_dv, start = kernel_call(
        functools.partial(grads_kernel, False), "grads_other", half, z, ins(other_k, other_v, half),
        [out, out, (sums, whole(sums))], [], 5 * keys * queries * HD, 8 * 2**20)
    own_dk, own_dv, dq = kernel_call(
        functools.partial(grads_kernel, True), "grads_own", half, z,
        ins(recv_k, recv_v, 0) + [(start, whole(start))],
        [out, out, (dq_shape, whole(dq_shape))],
        [pltpu.VMEM(sums.shape, sums.dtype)], 5 * keys * queries * HD, 8 * 2**20)
    return dq, (own_dk, own_dv), (other_dk, other_dv)


THIRDS = 3
SWAP = [(0, 1), (1, 0)]


def swap(array, axis):
    return lax.ppermute(array, axis, SWAP)


def along_z(pieces):
    count = len(pieces)
    routes = [[(i, (i + k) % count) for i in range(count)] for k in range(count)]
    return [pieces[0]] + [lax.ppermute(a, "z", route) for a, route in zip(pieces[1:], routes[1:])]


def over_chips(array):
    return lax.all_to_all(array, ("x", "y"), 0, 0, tiled=True)


def plane_at(place_ref, shift, count):
    return lax.rem(place_ref[0] + shift + count, count)


def split_kernel(place_ref, *refs):
    count = 4
    ins, outs = refs[:-count], refs[-count:]
    kinds = len(ins) // 2
    clips, tokens, width = ins[0].shape
    rows = tokens // 2
    core = place_ref[1]
    start = pl.multiple_of(core * rows, rows)
    for k, out in enumerate(outs):
        slot = plane_at(place_ref, k, count)
        part, clip = slot // clips, lax.rem(slot, clips)

        for mine, group in ((True, ins[:kinds]), (False, ins[kinds:])):
            @pl.when((part == core) == mine)
            def _(out=out, group=group, clip=clip):
                for index, ref in enumerate(group):
                    out[:, index * width:(index + 1) * width] = ref[clip, pl.ds(start, rows), :]


def keep_kernel(c_ref, *refs):
    out = refs[-1]
    kinds = len(refs) // 2
    clips, tokens, width = refs[0].shape
    rows = tokens // 2
    core = c_ref[0]
    start = pl.multiple_of(core * rows, rows)
    for part, group in ((core, refs[:kinds]), (1 - core, refs[kinds:2 * kinds])):
        for clip in range(clips):
            for index, ref in enumerate(group):
                out[part * clips + clip, :, index * width:(index + 1) * width] = ref[clip, pl.ds(start, rows), :]


def home_kernel(c_ref, back_ref, got_ref, *outs):
    clips, tokens, width = outs[0].shape
    rows = tokens // 2
    core = c_ref[0]
    for clip in range(clips):
        for index, out in enumerate(outs):
            lanes = slice(index * width, (index + 1) * width)
            out[clip, pl.ds(pl.multiple_of(core * rows, rows), rows), :] = back_ref[core * clips + clip, :, lanes]
            out[clip, pl.ds(pl.multiple_of((1 - core) * rows, rows), rows), :] = got_ref[core * clips + clip, :, lanes]


def keys_kernel(heads, z_ref, *refs):
    plane_ref, out = refs
    rows = plane_ref.shape[0]
    window = out.shape[1] - rows
    width = heads * HD
    for head in range(heads):
        for kind in range(4):
            source = slice(kind * width + head * HD, kind * width + (head + 1) * HD)
            lanes = slice((kind % 2) * HD, (kind % 2 + 1) * HD)
            whole_block = plane_ref[:, source]
            for third in range(THIRDS):
                chip = head * THIRDS + third
                if kind < 2:
                    out[chip, 0:rows, lanes] = whole_block
                else:
                    first = third * window
                    count = min(window, rows - first)
                    out[chip, rows:rows + count, lanes] = whole_block[first:first + count]
                    if count < window:
                        out[chip, rows + count:, lanes] = jnp.zeros((window - count, HD), out.dtype)
    for chip in range(heads * THIRDS, out.shape[0]):
        out[chip] = jnp.zeros(out.shape[1:], out.dtype)


def values_pack_kernel(heads, place_ref, *refs):
    ins, out, scr = refs[:-2], refs[-2], refs[-1]
    part = ins[0].shape[0]
    rows = part * len(ins)
    for k, ref in enumerate(ins):
        scr[pl.ds(pl.multiple_of(plane_at(place_ref, -k, len(ins)) * part, part), part), :] = ref[...]
    window = out.shape[1] - 2 * rows
    width = heads * HD
    for head in range(heads):
        for kind in range(3):
            source = slice(kind * width + head * HD, kind * width + (head + 1) * HD)
            whole_block = scr[:, source]
            for third in range(THIRDS):
                chip = head * THIRDS + third
                if kind < 2:
                    out[chip, kind * rows:(kind + 1) * rows, :] = whole_block
                else:
                    first = third * window
                    count = min(window, rows - first)
                    out[chip, 2 * rows:2 * rows + count, :] = whole_block[first:first + count]
                    if count < window:
                        out[chip, 2 * rows + count:, :] = jnp.zeros((window - count, HD), out.dtype)
    for chip in range(heads * THIRDS, out.shape[0]):
        out[chip] = jnp.zeros(out.shape[1:], out.dtype)


def out_unpack_kernel(heads, place_ref, back_ref, *refs):
    outs, scr = refs[:-1], refs[-1]
    part = outs[0].shape[0]
    window = back_ref.shape[1]
    rows = part * len(outs)
    width = heads * HD
    for head in range(heads):
        for kind in range(2):
            lanes = slice(kind * HD, (kind + 1) * HD)
            pieces = [
                back_ref[head * THIRDS + third, 0:min(window, rows - third * window), lanes]
                for third in range(THIRDS)
            ]
            scr[:, kind * width + head * HD:kind * width + (head + 1) * HD] = jnp.concatenate(pieces, axis=0)
    for k, out in enumerate(outs):
        out[...] = scr[pl.ds(pl.multiple_of(plane_at(place_ref, k, len(outs)) * part, part), part), :]


def join_out_kernel(place_ref, *refs):
    ins, own_ref, other_ref = refs[:-2], refs[-2], refs[-1]
    rows, width = ins[0].shape
    clips, width = len(ins) // 2, width // 2
    for k, ref in enumerate(ins):
        slot = plane_at(place_ref, -k, len(ins))
        part, clip = slot // clips, lax.rem(slot, clips)
        for mine, out in ((True, own_ref), (False, other_ref)):
            @pl.when((part == place_ref[1]) == mine)
            def _(ref=ref, out=out, clip=clip):
                for kind in range(2):
                    first = pl.multiple_of((kind * clips + clip) * rows, rows)
                    out[pl.ds(first, rows), :] = ref[:, kind * width:(kind + 1) * width]


def home_out_kernel(c_ref, keep_ref, got_ref, *outs):
    clips, tokens, width = outs[0].shape
    rows = tokens // 2
    core = c_ref[0]
    for ref, half in ((keep_ref, core), (got_ref, 1 - core)):
        for kind, out in enumerate(outs):
            for clip in range(clips):
                first = (kind * clips + clip) * rows
                lanes = pl.ds(pl.multiple_of(core * width, HD), width)
                out[clip, pl.ds(pl.multiple_of(half * rows, rows), rows), :] = ref[first:first + rows, lanes]


def grads_unpack_kernel(heads, z_ref, back_ref, out_ref):
    part = out_ref.shape[1]
    rows = part * out_ref.shape[0]
    window = back_ref.shape[1] - 2 * rows
    width = heads * HD
    for head in range(heads):
        for kind in range(3):
            chips = [head * THIRDS + third for third in range(THIRDS)]
            if kind < 2:
                column = sum(
                    back_ref[chip, kind * rows:(kind + 1) * rows, :].astype(jnp.float32) for chip in chips
                ).astype(jnp.bfloat16)
            else:
                column = jnp.concatenate([
                    back_ref[chip, 2 * rows:2 * rows + min(window, rows - third * window), :]
                    for third, chip in enumerate(chips)
                ], axis=0)
            for d in range(out_ref.shape[0]):
                lanes = slice(kind * width + head * HD, kind * width + (head + 1) * HD)
                out_ref[d, :, lanes] = column[d * part:(d + 1) * part]


def merge_kernel(z_ref, *refs):
    own, got, dq_ref, out_ref = refs[:2], refs[2:4], refs[4], refs[5]
    rows = own[0].shape[1]
    for kind in range(2):
        total = own[kind][...].astype(jnp.float32) + got[kind][...].astype(jnp.float32)
        out_ref[:, kind * rows:(kind + 1) * rows, :] = total.astype(jnp.bfloat16)
    out_ref[:, 2 * rows:, :] = dq_ref[...]


def repack(body, name, z, ins, shapes, scratch=(), limit=VMEM_LIMIT):
    shapes = [jax.ShapeDtypeStruct(s, jnp.bfloat16) for s in shapes]
    return kernel_call(body, name, 1, z, [(a, whole(a)) for a in ins], [(s, whole(s)) for s in shapes], list(scratch), limit=limit)


def over_planes(array):
    return lax.all_to_all(array, "z", 0, 0, tiled=True)


def local(queries, keys, values, queries_tan, keys_tan, values_tan, w_out, grad_out):
    w, c = lax.axis_index("w"), lax.axis_index("c")
    z = lax.axis_index("z").astype(jnp.int32).reshape(1)
    core = c.astype(jnp.int32).reshape(1)
    place = jnp.concatenate([z, core])
    clips, tokens, features = queries.shape
    heads = features // HD
    chips = lax.axis_size(("x", "y"))
    slots = 2 * clips
    rows = slots * tokens // 2
    window = pl.cdiv(pl.cdiv(rows, THIRDS), SUB) * SUB

    w_other = swap(w_out, "c")

    far = swap(grad_out, "w")
    near = swap(grad_out, "c")
    kinds = (keys, keys_tan, queries_tan, queries)
    got = tuple(swap(kind, "c") for kind in kinds)
    got_values = tuple(swap(kind, "c") for kind in (values, values_tan))
    kept = repack(keep_kernel, "keep_keys", core, kinds + got, [(slots, tokens // 2, len(kinds) * features)],
                  limit=60 * 2**20)[0]
    plane = over_planes(kept).reshape(rows, -1)
    cross = swap(far, "c")
    width = grad_out.shape[2]
    blocks = [
        lax.dynamic_slice_in_dim(w_out, ((w ^ i) * 2 + (c ^ j)) * width, width, axis=1)
        for i in range(2) for j in range(2)
    ]
    cot = sum(
        jnp.einsum("btf,cf->btc", grad, part, preferred_element_type=jnp.float32)
        for grad, part in zip((grad_out, near, far, cross), blocks)
    ).astype(jnp.bfloat16)
    kinds = (values, values_tan, cot)
    got = got_values + (swap(cot, "c"),)
    shape = (tokens // 2, len(kinds) * features)
    split = repack(split_kernel, "split_values", place, kinds + got, [shape] * slots)
    plane, split = lax.optimization_barrier((plane, split))
    plane_v = along_z(split)

    packed = repack(functools.partial(keys_kernel, heads), "pack_keys", z, [plane], [(chips, rows + window, 2 * HD)])[0]
    recv_k = over_chips(packed)
    recv_k, plane_v = lax.optimization_barrier((recv_k, plane_v))
    other_k = swap(recv_k, "c")
    packed = repack(functools.partial(values_pack_kernel, heads), "pack_values", place, plane_v, [(chips, 2 * rows + window, HD)],
                    [pltpu.VMEM((rows, 3 * features), jnp.bfloat16)])[0]
    recv_v = over_chips(packed)

    probs, weights = attention_weights(z, recv_k, other_k, rows, window)
    recv_v, probs, weights = lax.optimization_barrier((recv_v, probs, weights))
    other_v = swap(recv_v, "c")
    out, dsum = attention_values(z, recv_v, other_v, probs, weights, rows, window)
    back = over_chips(out)
    dq, own_grads, other_grads = attention_grads(z, recv_k, other_k, recv_v, other_v, probs, dsum, rows, window)
    back, other_grads = lax.optimization_barrier((back, other_grads))
    shape = (tokens // 2, 2 * features)
    home = along_z(repack(functools.partial(out_unpack_kernel, heads), "unpack_out", place, [back], [shape] * slots,
                          [pltpu.VMEM((rows, 2 * features), jnp.bfloat16)]))
    got = tuple(swap(grad, "c") for grad in other_grads)
    merged = repack(merge_kernel, "merge", z, own_grads + got + (dq,), [(chips, 2 * rows + window, HD)])[0]
    home, merged = lax.optimization_barrier((home, merged))
    grads = over_chips(merged)
    own, other = repack(join_out_kernel, "join_out", place, home, [(slots * tokens // 2, features)] * 2)

    def project(chip):
        parts = [
            jnp.dot(rows_of, lax.dynamic_slice_in_dim(weight, chip * 2 * width, 2 * width, axis=1),
                    preferred_element_type=jnp.float32)
            for rows_of, weight in ((own, w_out), (other, w_other))
        ]
        return parts[0] + parts[1]

    got = swap(project(1 - w).astype(jnp.bfloat16), "w")
    total = (project(w) + got.astype(jnp.float32)).astype(jnp.bfloat16)
    outs = repack(home_out_kernel, "home_out", core, [total, swap(total, "c")], [(clips, tokens, width)] * 2)

    shape = (slots, tokens // 2, 3 * features)
    back = over_planes(repack(functools.partial(grads_unpack_kernel, heads), "unpack_grads", z, [grads], [shape])[0])
    grad_k, grad_v, grad_q = repack(home_kernel, "home_grads", core, [back, swap(back, "c")], [queries.shape] * 3)
    return outs[0], outs[1], grad_q, grad_k, grad_v


def solution(mesh):
    seq, tp = ("x", "y", "z"), ("w", "c")
    fine = Mesh(mesh.devices.reshape(4, 4, 4, 2, 2), seq + tp)
    split = P(None, seq, tp)
    return jax.shard_map(
        local,
        mesh=fine,
        in_specs=(split,) * 6 + (P(tp, None), split),
        out_specs=(split,) * 5,
        check_vma=False,
    )
```

```python
import functools

import jax
import jax.numpy as jnp
from jax import lax
from jax.experimental import pallas as pl
from jax.experimental.pallas import tpu as pltpu
from jax.sharding import Mesh, PartitionSpec as P

HD = 128
SCALE = HD ** (-0.5)
LOG2E = 1.4426950408889634
SUB = 16
W_GROUP, W_UNROLL = 4, 4
V_GROUP = 8
G_GROUP = 8
VMEM_LIMIT = 52 * 2**20
NT = (((1,), (1,)), ((), ()))
NN = (((1,), (0,)), ((), ()))


def dot(a, b, dims=NN):
    return lax.dot_general(a, b, dims, preferred_element_type=jnp.float32)


def piece(ref, j, group, first, count, lanes=slice(None)):
    block = ref[pl.ds(j * group, group), first:first + count, lanes]
    return block.reshape(group * count, block.shape[-1])


def key_rows(half, j, group, blocks, rows):
    start = (half * blocks + j * group) * rows
    return pl.ds(pl.multiple_of(start, group * rows), group * rows)


def weights_kernel(rows, z_ref, q_ref, ka_ref, kb_ref, p_ref, w_ref, s_scr, t_scr):
    blocks = ka_ref.shape[0]
    tile = p_ref.shape[1]
    qtq = q_ref[...].reshape(tile, 2 * HD)
    q = qtq[:, HD:]

    top = jnp.full((1, tile), -jnp.inf, jnp.float32)
    for half, ref in enumerate((ka_ref, kb_ref)):
        def scores(j, top, half=half, ref=ref):
            here = key_rows(half, j, W_GROUP, blocks, rows)
            both = piece(ref, j, W_GROUP, 0, rows)
            s = dot(both[:, :HD], q, NT)
            s_scr[here, :] = s
            t_scr[here, :] = dot(both, qtq, NT)
            return jnp.maximum(top, jnp.max(s, axis=0, keepdims=True))
        top = lax.fori_loop(0, blocks // W_GROUP, scores, top, unroll=W_UNROLL)

    zero = jnp.zeros((1, tile), jnp.float32)

    def sums(j, carry):
        total, slope = carry
        here = key_rows(0, j, W_GROUP, blocks, rows)
        e = jnp.exp2((s_scr[here, :] - top) * (SCALE * LOG2E))
        s_scr[here, :] = e
        total += jnp.sum(e, axis=0, keepdims=True)
        slope += jnp.sum(e * t_scr[here, :], axis=0, keepdims=True)
        return total, slope

    total, slope = lax.fori_loop(0, 2 * blocks // W_GROUP, sums, (zero, zero), unroll=W_UNROLL)
    inv = 1.0 / total
    slope = slope * inv

    def store(j, carry):
        here = key_rows(0, j, W_GROUP, blocks, rows)
        p = s_scr[here, :] * inv
        p_ref[here, :] = p.astype(jnp.bfloat16)
        w_ref[here, :] = (p * (t_scr[here, :] - slope)).astype(jnp.bfloat16)
        return carry

    lax.fori_loop(0, 2 * blocks // W_GROUP, store, 0, unroll=W_UNROLL)


def window_rows(refs):
    return jnp.concatenate([ref[...].reshape(-1, HD) for ref in refs], axis=0)


def put_rows(ref, lanes, value, first=0):
    blocks, height, _ = ref.shape
    tile = blocks * SUB
    for i in range((height - first) // SUB):
        ref[:, first + i * SUB:first + (i + 1) * SUB, lanes] = value[i * tile:(i + 1) * tile].astype(ref.dtype).reshape(blocks, SUB, HD)


def values_kernel(last, z_ref, v_ref, t_ref, p_ref, w_ref, *refs):
    step = pl.program_id(0)
    if last:
        *g_refs, start_ref, out_ref, d_ref, acc = refs
    else:
        acc = refs[0]
    chunk = p_ref.shape[0]
    v = v_ref[...].reshape(chunk, HD)
    both = jnp.concatenate([v, t_ref[...].reshape(chunk, HD)], axis=1).T

    @pl.when(step == 0)
    def _():
        acc[...] = start_ref[...] if last else jnp.zeros_like(acc)

    acc[0:2 * HD, :] += dot(both, p_ref[...])
    acc[2 * HD:, :] += dot(both[0:HD], w_ref[...])

    if last:
        @pl.when(step == pl.num_programs(0) - 1)
        def _():
            g = window_rows(g_refs).astype(jnp.float32)
            attn = acc[0:HD, :].T.astype(jnp.bfloat16)
            dsum = jnp.sum(attn.astype(jnp.float32) * g, axis=1, keepdims=True)
            d_ref[...] = jnp.broadcast_to(dsum, (dsum.shape[0], HD)).T[0:1, :]
            tan = acc[HD:2 * HD, :] + SCALE * acc[2 * HD:, :]
            put_rows(out_ref, slice(0, HD), attn)
            put_rows(out_ref, slice(HD, 2 * HD), tan.T)


def grads_kernel(last, z_ref, k_ref, v_ref, p_ref, d_ref, *refs):
    step = pl.program_id(0)
    chunk, queries = p_ref.shape
    count = (len(refs) - (5 if last else 3)) // 2
    q, g, refs = window_rows(refs[:count]), window_rows(refs[count:2 * count]), refs[2 * count:]
    if last:
        start_ref, got_k_ref, got_v_ref, out_ref, acc = refs
    else:
        dk_ref, dv_ref, acc = refs
    k = k_ref[...].reshape(chunk, HD)
    v = v_ref[...].reshape(chunk, HD)
    p = p_ref[...]

    @pl.when(step == 0)
    def _():
        acc[...] = start_ref[...] if last else jnp.zeros_like(acc)

    ds = (p.astype(jnp.float32) * (dot(v, g, NT) - d_ref[...])).astype(jnp.bfloat16)
    dk = (SCALE * dot(ds, q)).reshape(k_ref.shape)
    dv = dot(p, g).reshape(k_ref.shape)
    acc[...] += dot(k.T, ds)

    if last:
        blocks, rows, _ = k_ref.shape
        group = pl.ds(step * blocks, blocks)
        out_ref[group, 0:rows, :] = (dk + got_k_ref[...].astype(jnp.float32)).astype(jnp.bfloat16)
        out_ref[group, rows:2 * rows, :] = (dv + got_v_ref[...].astype(jnp.float32)).astype(jnp.bfloat16)

        @pl.when(step == pl.num_programs(0) - 1)
        def _():
            put_rows(out_ref, slice(0, HD), (SCALE * acc[...]).T, 2 * rows)
    else:
        dk_ref[...] = dk.astype(jnp.bfloat16)
        dv_ref[...] = dv.astype(jnp.bfloat16)


def whole(array):
    return pl.BlockSpec(array.shape, lambda i, s: (0,) * len(array.shape))


def kernel_call(body, name, grid, scalars, ins, outs, scratch, flops=0, bytes_accessed=4 * 2**20, limit=VMEM_LIMIT):
    arrays, in_specs = zip(*ins)
    shapes, out_specs = zip(*outs)
    return pl.pallas_call(
        body,
        grid_spec=pltpu.PrefetchScalarGridSpec(
            num_scalar_prefetch=1,
            grid=(grid,),
            in_specs=list(in_specs),
            out_specs=list(out_specs),
            scratch_shapes=scratch,
        ),
        out_shape=list(shapes),
        name=name,
        compiler_params=pltpu.CompilerParams(vmem_limit_bytes=limit),
        cost_estimate=pl.CostEstimate(flops=flops, bytes_accessed=bytes_accessed, transcendentals=0),
    )(scalars, *arrays)


def specs(blocks, rows, window):
    tile = blocks * SUB
    keys = 2 * blocks * rows
    q_spec = pl.BlockSpec((blocks, SUB, 2 * HD), lambda i, s: (0, rows // SUB + i, 0))
    g_spec = pl.BlockSpec((blocks, SUB, HD), lambda i, s: (0, 2 * rows // SUB + i, 0))
    p_spec = pl.BlockSpec((keys, tile), lambda i, s: (0, i))
    d_spec = pl.BlockSpec((1, tile), lambda i, s: (0, i))
    return q_spec, g_spec, p_spec, d_spec, keys, tile, window // SUB


def attention_weights(z, recv_k, other_k, rows, window):
    q_spec, _, p_spec, _, keys, tile, grid = specs(recv_k.shape[0], rows, window)
    p_shape = jax.ShapeDtypeStruct((keys, grid * tile), jnp.bfloat16)
    return kernel_call(
        functools.partial(weights_kernel, rows), "weights", grid, z,
        [(recv_k, q_spec), (recv_k, whole(recv_k)), (other_k, whole(other_k))],
        [(p_shape, p_spec), (p_shape, p_spec)],
        [pltpu.VMEM((keys, tile), jnp.float32), pltpu.VMEM((keys, tile), jnp.float32)],
        8 * keys * grid * tile * HD, 32 * 2**20)


def windows(array, first, window, lane):
    blocks = array.shape[0]
    return [
        (array, pl.BlockSpec((blocks, SUB, HD), lambda i, s, at=first // SUB + part: (0, at, lane)))
        for part in range(window // SUB)
    ]


def attention_values(z, recv_v, other_v, probs, weights, rows, window):
    blocks = recv_v.shape[0]
    keys, queries = probs.shape
    half = blocks // V_GROUP
    sums = jax.ShapeDtypeStruct((3 * HD, queries), jnp.float32)
    out_shape = jax.ShapeDtypeStruct((blocks, window, 2 * HD), jnp.bfloat16)
    d_shape = jax.ShapeDtypeStruct((1, queries), jnp.float32)

    def ins(array, first):
        p_spec = pl.BlockSpec((V_GROUP * rows, queries), lambda i, s: (first + i, 0))
        return [
            (array, pl.BlockSpec((V_GROUP, rows, HD), lambda i, s: (i, 0, 0))),
            (array, pl.BlockSpec((V_GROUP, rows, HD), lambda i, s: (i, 1, 0))),
            (probs, p_spec), (weights, p_spec),
        ]

    start = kernel_call(
        functools.partial(values_kernel, False), "values_own", half, z, ins(recv_v, 0),
        [(sums, whole(sums))], [], 3 * keys * queries * HD, 8 * 2**20)[0]
    g = windows(recv_v, 2 * rows, window, 0)
    return kernel_call(
        functools.partial(values_kernel, True), "values_other", half, z,
        ins(other_v, half) + g + [(start, whole(start))],
        [(out_shape, whole(out_shape)), (d_shape, whole(d_shape))],
        [pltpu.VMEM(sums.shape, sums.dtype)], 3 * keys * queries * HD, 8 * 2**20)


def attention_grads(z, recv_k, other_k, recv_v, other_v, probs, dsum, rows, window):
    blocks = recv_v.shape[0]
    keys, queries = probs.shape
    half = blocks // G_GROUP
    shape = jax.ShapeDtypeStruct((blocks, rows, HD), jnp.bfloat16)
    merged = jax.ShapeDtypeStruct((blocks, 2 * rows + window, HD), jnp.bfloat16)
    sums = jax.ShapeDtypeStruct((HD, queries), jnp.float32)
    block = pl.BlockSpec((G_GROUP, rows, HD), lambda i, s: (i, 0, 0))

    def ins(k, v, first):
        return [
            (k, block), (v, block),
            (probs, pl.BlockSpec((G_GROUP * rows, queries), lambda i, s: (first + i, 0))),
            (dsum, whole(dsum)),
        ] + windows(recv_k, rows, window, 1) + windows(recv_v, 2 * rows, window, 0)

    other_dk, other_dv, start = kernel_call(
        functools.partial(grads_kernel, False), "grads_other", half, z, ins(other_k, other_v, half),
        [(shape, block), (shape, block), (sums, whole(sums))], [], 5 * keys * queries * HD, 8 * 2**20)

    def own(got):
        return kernel_call(
            functools.partial(grads_kernel, True), "grads_own", half, z,
            ins(recv_k, recv_v, 0) + [(start, whole(start)), (got[0], block), (got[1], block)],
            [(merged, whole(merged))], [pltpu.VMEM(sums.shape, sums.dtype)], 5 * keys * queries * HD, 8 * 2**20)[0]

    return (other_dk, other_dv), own


THIRDS = 3
SWAP = [(0, 1), (1, 0)]


def swap(array, axis):
    return lax.ppermute(array, axis, SWAP)


def along_z(pieces):
    count = len(pieces)
    routes = [[(i, (i + k) % count) for i in range(count)] for k in range(count)]
    return [pieces[0]] + [lax.ppermute(a, "z", route) for a, route in zip(pieces[1:], routes[1:])]


def over_chips(array):
    return lax.all_to_all(array, ("x", "y"), 0, 0, tiled=True)


def plane_at(place_ref, shift, count):
    return lax.rem(place_ref[0] + shift + count, count)


def split_kernel(place_ref, *refs):
    count = 4
    ins, outs = refs[:-count], refs[-count:]
    kinds = len(ins) // 2
    clips, tokens, width = ins[0].shape
    rows = tokens // 2
    core = place_ref[1]
    start = pl.multiple_of(core * rows, rows)
    for k, out in enumerate(outs):
        slot = plane_at(place_ref, k, count)
        part, clip = slot // clips, lax.rem(slot, clips)

        for mine, group in ((True, ins[:kinds]), (False, ins[kinds:])):
            @pl.when((part == core) == mine)
            def _(out=out, group=group, clip=clip):
                for index, ref in enumerate(group):
                    out[:, index * width:(index + 1) * width] = ref[clip, pl.ds(start, rows), :]


def keep_kernel(c_ref, *refs):
    out = refs[-1]
    kinds = len(refs) // 2
    clips, tokens, width = refs[0].shape
    rows = tokens // 2
    core = c_ref[0]
    start = pl.multiple_of(core * rows, rows)
    for part, group in ((core, refs[:kinds]), (1 - core, refs[kinds:2 * kinds])):
        for clip in range(clips):
            for index, ref in enumerate(group):
                out[part * clips + clip, :, index * width:(index + 1) * width] = ref[clip, pl.ds(start, rows), :]


def home_kernel(c_ref, back_ref, got_ref, *outs):
    clips, tokens, width = outs[0].shape
    rows = tokens // 2
    core = c_ref[0]
    for clip in range(clips):
        for index, out in enumerate(outs):
            lanes = slice(index * width, (index + 1) * width)
            out[clip, pl.ds(pl.multiple_of(core * rows, rows), rows), :] = back_ref[core * clips + clip, :, lanes]
            out[clip, pl.ds(pl.multiple_of((1 - core) * rows, rows), rows), :] = got_ref[core * clips + clip, :, lanes]


def keys_kernel(heads, z_ref, *refs):
    plane_ref, out = refs
    rows = plane_ref.shape[0]
    window = out.shape[1] - rows
    width = heads * HD
    for head in range(heads):
        for kind in range(4):
            source = slice(kind * width + head * HD, kind * width + (head + 1) * HD)
            lanes = slice((kind % 2) * HD, (kind % 2 + 1) * HD)
            whole_block = plane_ref[:, source]
            for third in range(THIRDS):
                chip = head * THIRDS + third
                if kind < 2:
                    out[chip, 0:rows, lanes] = whole_block
                else:
                    first = third * window
                    count = min(window, rows - first)
                    out[chip, rows:rows + count, lanes] = whole_block[first:first + count]
                    if count < window:
                        out[chip, rows + count:, lanes] = jnp.zeros((window - count, HD), out.dtype)
    for chip in range(heads * THIRDS, out.shape[0]):
        out[chip] = jnp.zeros(out.shape[1:], out.dtype)


def values_pack_kernel(heads, place_ref, *refs):
    ins, out, scr = refs[:-2], refs[-2], refs[-1]
    part = ins[0].shape[0]
    rows = part * len(ins)
    for k, ref in enumerate(ins):
        scr[pl.ds(pl.multiple_of(plane_at(place_ref, -k, len(ins)) * part, part), part), :] = ref[...]
    window = out.shape[1] - 2 * rows
    width = heads * HD
    for head in range(heads):
        for kind in range(3):
            source = slice(kind * width + head * HD, kind * width + (head + 1) * HD)
            whole_block = scr[:, source]
            for third in range(THIRDS):
                chip = head * THIRDS + third
                if kind < 2:
                    out[chip, kind * rows:(kind + 1) * rows, :] = whole_block
                else:
                    first = third * window
                    count = min(window, rows - first)
                    out[chip, 2 * rows:2 * rows + count, :] = whole_block[first:first + count]
                    if count < window:
                        out[chip, 2 * rows + count:, :] = jnp.zeros((window - count, HD), out.dtype)
    for chip in range(heads * THIRDS, out.shape[0]):
        out[chip] = jnp.zeros(out.shape[1:], out.dtype)


def out_unpack_kernel(heads, place_ref, back_ref, *refs):
    outs, scr = refs[:-1], refs[-1]
    part = outs[0].shape[0]
    window = back_ref.shape[1]
    rows = part * len(outs)
    width = heads * HD
    for head in range(heads):
        for kind in range(2):
            lanes = slice(kind * HD, (kind + 1) * HD)
            pieces = [
                back_ref[head * THIRDS + third, 0:min(window, rows - third * window), lanes]
                for third in range(THIRDS)
            ]
            scr[:, kind * width + head * HD:kind * width + (head + 1) * HD] = jnp.concatenate(pieces, axis=0)
    for k, out in enumerate(outs):
        out[...] = scr[pl.ds(pl.multiple_of(plane_at(place_ref, k, len(outs)) * part, part), part), :]


def join_out_kernel(place_ref, *refs):
    ins, own_ref, other_ref = refs[:-2], refs[-2], refs[-1]
    rows, width = ins[0].shape
    clips, width = len(ins) // 2, width // 2
    for k, ref in enumerate(ins):
        slot = plane_at(place_ref, -k, len(ins))
        part, clip = slot // clips, lax.rem(slot, clips)
        for mine, out in ((True, own_ref), (False, other_ref)):
            @pl.when((part == place_ref[1]) == mine)
            def _(ref=ref, out=out, clip=clip):
                for kind in range(2):
                    first = pl.multiple_of((kind * clips + clip) * rows, rows)
                    out[pl.ds(first, rows), :] = ref[:, kind * width:(kind + 1) * width]


def home_out_kernel(c_ref, keep_ref, got_ref, *outs):
    clips, tokens, width = outs[0].shape
    rows = tokens // 2
    core = c_ref[0]
    for ref, half in ((keep_ref, core), (got_ref, 1 - core)):
        for kind, out in enumerate(outs):
            for clip in range(clips):
                first = (kind * clips + clip) * rows
                lanes = pl.ds(pl.multiple_of(core * width, HD), width)
                out[clip, pl.ds(pl.multiple_of(half * rows, rows), rows), :] = ref[first:first + rows, lanes]


def grads_unpack_kernel(heads, z_ref, back_ref, out_ref):
    part = out_ref.shape[1]
    rows = part * out_ref.shape[0]
    window = back_ref.shape[1] - 2 * rows
    width = heads * HD
    for head in range(heads):
        for kind in range(3):
            chips = [head * THIRDS + third for third in range(THIRDS)]
            if kind < 2:
                column = sum(
                    back_ref[chip, kind * rows:(kind + 1) * rows, :].astype(jnp.float32) for chip in chips
                ).astype(jnp.bfloat16)
            else:
                column = jnp.concatenate([
                    back_ref[chip, 2 * rows:2 * rows + min(window, rows - third * window), :]
                    for third, chip in enumerate(chips)
                ], axis=0)
            for d in range(out_ref.shape[0]):
                lanes = slice(kind * width + head * HD, kind * width + (head + 1) * HD)
                out_ref[d, :, lanes] = column[d * part:(d + 1) * part]


def repack(body, name, z, ins, shapes, scratch=(), limit=20 * 2**20):
    shapes = [jax.ShapeDtypeStruct(s, jnp.bfloat16) for s in shapes]
    return kernel_call(body, name, 1, z, [(a, whole(a)) for a in ins], [(s, whole(s)) for s in shapes], list(scratch), limit=limit)


def over_planes(array):
    return lax.all_to_all(array, "z", 0, 0, tiled=True)


def local(queries, keys, values, queries_tan, keys_tan, values_tan, w_out, grad_out):
    w, c = lax.axis_index("w"), lax.axis_index("c")
    z = lax.axis_index("z").astype(jnp.int32).reshape(1)
    core = c.astype(jnp.int32).reshape(1)
    place = jnp.concatenate([z, core])
    clips, tokens, features = queries.shape
    heads = features // HD
    chips = lax.axis_size(("x", "y"))
    slots = 2 * clips
    rows = slots * tokens // 2
    window = pl.cdiv(pl.cdiv(rows, THIRDS), SUB) * SUB

    w_other = swap(w_out, "c")

    far = swap(grad_out, "w")
    near = swap(grad_out, "c")
    kinds = (keys, keys_tan, queries_tan, queries)
    got = tuple(swap(kind, "c") for kind in kinds)
    got_values = tuple(swap(kind, "c") for kind in (values, values_tan))
    kept = repack(keep_kernel, "keep_keys", core, kinds + got, [(slots, tokens // 2, len(kinds) * features)],
                  limit=60 * 2**20)[0]
    plane = over_planes(kept).reshape(rows, -1)
    cross = swap(far, "c")
    width = grad_out.shape[2]
    blocks = [
        lax.dynamic_slice_in_dim(w_out, ((w ^ i) * 2 + (c ^ j)) * width, width, axis=1)
        for i in range(2) for j in range(2)
    ]
    cot = sum(
        jnp.einsum("btf,cf->btc", grad, part, preferred_element_type=jnp.float32)
        for grad, part in zip((grad_out, near, far, cross), blocks)
    ).astype(jnp.bfloat16)
    kinds = (values, values_tan, cot)
    got = got_values + (swap(cot, "c"),)
    shape = (tokens // 2, len(kinds) * features)
    split = repack(split_kernel, "split_values", place, kinds + got, [shape] * slots)
    plane, split = lax.optimization_barrier((plane, split))
    plane_v = along_z(split)

    packed = repack(functools.partial(keys_kernel, heads), "pack_keys", z, [plane], [(chips, rows + window, 2 * HD)])[0]
    recv_k = over_chips(packed)
    recv_k, plane_v = lax.optimization_barrier((recv_k, plane_v))
    other_k = swap(recv_k, "c")
    packed = repack(functools.partial(values_pack_kernel, heads), "pack_values", place, plane_v, [(chips, 2 * rows + window, HD)],
                    [pltpu.VMEM((rows, 3 * features), jnp.bfloat16)])[0]
    recv_v = over_chips(packed)

    probs, weights = attention_weights(z, recv_k, other_k, rows, window)
    recv_v, probs, weights = lax.optimization_barrier((recv_v, probs, weights))
    other_v = swap(recv_v, "c")
    out, dsum = attention_values(z, recv_v, other_v, probs, weights, rows, window)
    back = over_chips(out)
    other_grads, own_half = attention_grads(z, recv_k, other_k, recv_v, other_v, probs, dsum, rows, window)
    back, other_grads = lax.optimization_barrier((back, other_grads))
    shape = (tokens // 2, 2 * features)
    home = along_z(repack(functools.partial(out_unpack_kernel, heads), "unpack_out", place, [back], [shape] * slots,
                          [pltpu.VMEM((rows, 2 * features), jnp.bfloat16)]))
    got = tuple(swap(grad, "c") for grad in other_grads)
    merged = own_half(got)
    home, merged = lax.optimization_barrier((home, merged))
    grads = over_chips(merged)
    own, other = repack(join_out_kernel, "join_out", place, home, [(slots * tokens // 2, features)] * 2)

    def project(chip):
        parts = [
            jnp.dot(rows_of, lax.dynamic_slice_in_dim(weight, chip * 2 * width, 2 * width, axis=1),
                    preferred_element_type=jnp.float32)
            for rows_of, weight in ((own, w_out), (other, w_other))
        ]
        return parts[0] + parts[1]

    got = swap(project(1 - w).astype(jnp.bfloat16), "w")
    total = (project(w) + got.astype(jnp.float32)).astype(jnp.bfloat16)
    outs = repack(home_out_kernel, "home_out", core, [total, swap(total, "c")], [(clips, tokens, width)] * 2)

    shape = (slots, tokens // 2, 3 * features)
    back = over_planes(repack(functools.partial(grads_unpack_kernel, heads), "unpack_grads", z, [grads], [shape])[0])
    grad_k, grad_v, grad_q = repack(home_kernel, "home_grads", core, [back, swap(back, "c")], [queries.shape] * 3)
    return outs[0], outs[1], grad_q, grad_k, grad_v


def solution(mesh):
    seq, tp = ("x", "y", "z"), ("w", "c")
    fine = Mesh(mesh.devices.reshape(4, 4, 4, 2, 2), seq + tp)
    split = P(None, seq, tp)
    return jax.shard_map(
        local,
        mesh=fine,
        in_specs=(split,) * 6 + (P(tp, None), split),
        out_specs=(split,) * 5,
        check_vma=False,
    )
```

```python
import functools

import jax
import jax.numpy as jnp
from jax import lax
from jax.experimental import pallas as pl
from jax.experimental.pallas import tpu as pltpu
from jax.sharding import Mesh, PartitionSpec as P

HD = 128
SCALE = HD ** (-0.5)
LOG2E = 1.4426950408889634
SUB = 16
W_GROUP, W_UNROLL = 4, 4
V_GROUP = 8
G_GROUP = 16
VMEM_LIMIT = 52 * 2**20
NT = (((1,), (1,)), ((), ()))
NN = (((1,), (0,)), ((), ()))


def dot(a, b, dims=NN):
    return lax.dot_general(a, b, dims, preferred_element_type=jnp.float32)


def piece(ref, j, group, first, count, lanes=slice(None)):
    block = ref[pl.ds(j * group, group), first:first + count, lanes]
    return block.reshape(group * count, block.shape[-1])


def key_rows(half, j, group, blocks, rows):
    start = (half * blocks + j * group) * rows
    return pl.ds(pl.multiple_of(start, group * rows), group * rows)


def weights_kernel(rows, z_ref, q_ref, ka_ref, kb_ref, p_ref, w_ref, s_scr, t_scr):
    blocks = ka_ref.shape[0]
    tile = p_ref.shape[1]
    qtq = q_ref[...].reshape(tile, 2 * HD)
    q = qtq[:, HD:]

    top = jnp.full((1, tile), -jnp.inf, jnp.float32)
    for half, ref in enumerate((ka_ref, kb_ref)):
        def scores(j, top, half=half, ref=ref):
            here = key_rows(half, j, W_GROUP, blocks, rows)
            both = piece(ref, j, W_GROUP, 0, rows)
            s = dot(both[:, :HD], q, NT)
            s_scr[here, :] = s
            t_scr[here, :] = dot(both, qtq, NT)
            return jnp.maximum(top, jnp.max(s, axis=0, keepdims=True))
        top = lax.fori_loop(0, blocks // W_GROUP, scores, top, unroll=W_UNROLL)

    zero = jnp.zeros((1, tile), jnp.float32)

    def sums(j, carry):
        total, slope = carry
        here = key_rows(0, j, W_GROUP, blocks, rows)
        e = jnp.exp2((s_scr[here, :] - top) * (SCALE * LOG2E))
        s_scr[here, :] = e
        total += jnp.sum(e, axis=0, keepdims=True)
        slope += jnp.sum(e * t_scr[here, :], axis=0, keepdims=True)
        return total, slope

    total, slope = lax.fori_loop(0, 2 * blocks // W_GROUP, sums, (zero, zero), unroll=W_UNROLL)
    inv = 1.0 / total
    slope = slope * inv

    def store(j, carry):
        here = key_rows(0, j, W_GROUP, blocks, rows)
        p = s_scr[here, :] * inv
        p_ref[here, :] = p.astype(jnp.bfloat16)
        w_ref[here, :] = (p * (t_scr[here, :] - slope)).astype(jnp.bfloat16)
        return carry

    lax.fori_loop(0, 2 * blocks // W_GROUP, store, 0, unroll=W_UNROLL)


def window_rows(refs):
    return jnp.concatenate([ref[...].reshape(-1, HD) for ref in refs], axis=0)


def put_rows(ref, lanes, value, first=0):
    blocks, height, _ = ref.shape
    tile = blocks * SUB
    for i in range((height - first) // SUB):
        ref[:, first + i * SUB:first + (i + 1) * SUB, lanes] = value[i * tile:(i + 1) * tile].astype(ref.dtype).reshape(blocks, SUB, HD)


def values_kernel(last, z_ref, v_ref, t_ref, p_ref, w_ref, *refs):
    step = pl.program_id(0)
    if last:
        *g_refs, start_ref, out_ref, d_ref, acc = refs
    else:
        acc = refs[0]
    chunk = p_ref.shape[0]
    v = v_ref[...].reshape(chunk, HD)
    both = jnp.concatenate([v, t_ref[...].reshape(chunk, HD)], axis=1).T

    @pl.when(step == 0)
    def _():
        acc[...] = start_ref[...] if last else jnp.zeros_like(acc)

    acc[0:2 * HD, :] += dot(both, p_ref[...])
    acc[2 * HD:, :] += dot(both[0:HD], w_ref[...])

    if last:
        @pl.when(step == pl.num_programs(0) - 1)
        def _():
            g = window_rows(g_refs).astype(jnp.float32)
            attn = acc[0:HD, :].T.astype(jnp.bfloat16)
            dsum = jnp.sum(attn.astype(jnp.float32) * g, axis=1, keepdims=True)
            d_ref[...] = jnp.broadcast_to(dsum, (dsum.shape[0], HD)).T[0:1, :]
            tan = acc[HD:2 * HD, :] + SCALE * acc[2 * HD:, :]
            put_rows(out_ref, slice(0, HD), attn)
            put_rows(out_ref, slice(HD, 2 * HD), tan.T)


def grads_kernel(last, z_ref, k_ref, v_ref, p_ref, d_ref, *refs):
    step = pl.program_id(0)
    chunk, queries = p_ref.shape
    count = (len(refs) - (5 if last else 3)) // 2
    q, g, refs = window_rows(refs[:count]), window_rows(refs[count:2 * count]), refs[2 * count:]
    if last:
        start_ref, got_k_ref, got_v_ref, out_ref, acc = refs
    else:
        dk_ref, dv_ref, acc = refs
    k = k_ref[...].reshape(chunk, HD)
    v = v_ref[...].reshape(chunk, HD)
    p = p_ref[...]

    @pl.when(step == 0)
    def _():
        acc[...] = start_ref[...] if last else jnp.zeros_like(acc)

    ds = (p.astype(jnp.float32) * (dot(v, g, NT) - d_ref[...])).astype(jnp.bfloat16)
    dk = (SCALE * dot(ds, q)).reshape(k_ref.shape)
    dv = dot(p, g).reshape(k_ref.shape)
    acc[...] += dot(k.T, ds)

    if last:
        blocks, rows, _ = k_ref.shape
        group = pl.ds(step * blocks, blocks)
        out_ref[group, 0:rows, :] = (dk + got_k_ref[...].astype(jnp.float32)).astype(jnp.bfloat16)
        out_ref[group, rows:2 * rows, :] = (dv + got_v_ref[...].astype(jnp.float32)).astype(jnp.bfloat16)

        @pl.when(step == pl.num_programs(0) - 1)
        def _():
            put_rows(out_ref, slice(0, HD), (SCALE * acc[...]).T, 2 * rows)
    else:
        dk_ref[...] = dk.astype(jnp.bfloat16)
        dv_ref[...] = dv.astype(jnp.bfloat16)


def whole(array):
    return pl.BlockSpec(array.shape, lambda i, s: (0,) * len(array.shape))


def kernel_call(body, name, grid, scalars, ins, outs, scratch, flops=0, bytes_accessed=4 * 2**20, limit=VMEM_LIMIT):
    arrays, in_specs = zip(*ins)
    shapes, out_specs = zip(*outs)
    return pl.pallas_call(
        body,
        grid_spec=pltpu.PrefetchScalarGridSpec(
            num_scalar_prefetch=1,
            grid=(grid,),
            in_specs=list(in_specs),
            out_specs=list(out_specs),
            scratch_shapes=scratch,
        ),
        out_shape=list(shapes),
        name=name,
        compiler_params=pltpu.CompilerParams(vmem_limit_bytes=limit),
        cost_estimate=pl.CostEstimate(flops=flops, bytes_accessed=bytes_accessed, transcendentals=0),
    )(scalars, *arrays)


def specs(blocks, rows, window):
    tile = blocks * SUB
    keys = 2 * blocks * rows
    q_spec = pl.BlockSpec((blocks, SUB, 2 * HD), lambda i, s: (0, rows // SUB + i, 0))
    g_spec = pl.BlockSpec((blocks, SUB, HD), lambda i, s: (0, 2 * rows // SUB + i, 0))
    p_spec = pl.BlockSpec((keys, tile), lambda i, s: (0, i))
    d_spec = pl.BlockSpec((1, tile), lambda i, s: (0, i))
    return q_spec, g_spec, p_spec, d_spec, keys, tile, window // SUB


def attention_weights(z, recv_k, other_k, rows, window):
    q_spec, _, p_spec, _, keys, tile, grid = specs(recv_k.shape[0], rows, window)
    p_shape = jax.ShapeDtypeStruct((keys, grid * tile), jnp.bfloat16)
    return kernel_call(
        functools.partial(weights_kernel, rows), "weights", grid, z,
        [(recv_k, q_spec), (recv_k, whole(recv_k)), (other_k, whole(other_k))],
        [(p_shape, p_spec), (p_shape, p_spec)],
        [pltpu.VMEM((keys, tile), jnp.float32), pltpu.VMEM((keys, tile), jnp.float32)],
        8 * keys * grid * tile * HD, 32 * 2**20)


def windows(array, first, window, lane):
    blocks = array.shape[0]
    return [
        (array, pl.BlockSpec((blocks, SUB, HD), lambda i, s, at=first // SUB + part: (0, at, lane)))
        for part in range(window // SUB)
    ]


def attention_values(z, recv_v, other_v, probs, weights, rows, window):
    blocks = recv_v.shape[0]
    keys, queries = probs.shape
    half = blocks // V_GROUP
    sums = jax.ShapeDtypeStruct((3 * HD, queries), jnp.float32)
    out_shape = jax.ShapeDtypeStruct((blocks, window, 2 * HD), jnp.bfloat16)
    d_shape = jax.ShapeDtypeStruct((1, queries), jnp.float32)

    def ins(array, first):
        p_spec = pl.BlockSpec((V_GROUP * rows, queries), lambda i, s: (first + i, 0))
        return [
            (array, pl.BlockSpec((V_GROUP, rows, HD), lambda i, s: (i, 0, 0))),
            (array, pl.BlockSpec((V_GROUP, rows, HD), lambda i, s: (i, 1, 0))),
            (probs, p_spec), (weights, p_spec),
        ]

    start = kernel_call(
        functools.partial(values_kernel, False), "values_own", half, z, ins(recv_v, 0),
        [(sums, whole(sums))], [], 3 * keys * queries * HD, 8 * 2**20)[0]
    g = windows(recv_v, 2 * rows, window, 0)
    return kernel_call(
        functools.partial(values_kernel, True), "values_other", half, z,
        ins(other_v, half) + g + [(start, whole(start))],
        [(out_shape, whole(out_shape)), (d_shape, whole(d_shape))],
        [pltpu.VMEM(sums.shape, sums.dtype)], 3 * keys * queries * HD, 8 * 2**20)


def attention_grads(z, recv_k, other_k, recv_v, other_v, probs, dsum, rows, window):
    blocks = recv_v.shape[0]
    keys, queries = probs.shape
    half = blocks // G_GROUP
    shape = jax.ShapeDtypeStruct((blocks, rows, HD), jnp.bfloat16)
    merged = jax.ShapeDtypeStruct((blocks, 2 * rows + window, HD), jnp.bfloat16)
    sums = jax.ShapeDtypeStruct((HD, queries), jnp.float32)
    block = pl.BlockSpec((G_GROUP, rows, HD), lambda i, s: (i, 0, 0))

    def ins(k, v, first):
        return [
            (k, block), (v, block),
            (probs, pl.BlockSpec((G_GROUP * rows, queries), lambda i, s: (first + i, 0))),
            (dsum, whole(dsum)),
        ] + windows(recv_k, rows, window, 1) + windows(recv_v, 2 * rows, window, 0)

    other_dk, other_dv, start = kernel_call(
        functools.partial(grads_kernel, False), "grads_other", half, z, ins(other_k, other_v, half),
        [(shape, block), (shape, block), (sums, whole(sums))], [], 5 * keys * queries * HD, 8 * 2**20)

    def own(got):
        return kernel_call(
            functools.partial(grads_kernel, True), "grads_own", half, z,
            ins(recv_k, recv_v, 0) + [(start, whole(start)), (got[0], block), (got[1], block)],
            [(merged, whole(merged))], [pltpu.VMEM(sums.shape, sums.dtype)], 5 * keys * queries * HD, 8 * 2**20)[0]

    return (other_dk, other_dv), own


THIRDS = 3
SWAP = [(0, 1), (1, 0)]


def swap(array, axis):
    return lax.ppermute(array, axis, SWAP)


def along_z(pieces):
    count = len(pieces)
    routes = [[(i, (i + k) % count) for i in range(count)] for k in range(count)]
    return [pieces[0]] + [lax.ppermute(a, "z", route) for a, route in zip(pieces[1:], routes[1:])]


def over_chips(array):
    return lax.all_to_all(array, ("x", "y"), 0, 0, tiled=True)


def plane_at(place_ref, shift, count):
    return lax.rem(place_ref[0] + shift + count, count)


def split_kernel(place_ref, *refs):
    count = 4
    ins, outs = refs[:-count], refs[-count:]
    kinds = len(ins) // 2
    clips, tokens, width = ins[0].shape
    rows = tokens // 2
    core = place_ref[1]
    start = pl.multiple_of(core * rows, rows)
    for k, out in enumerate(outs):
        slot = plane_at(place_ref, k, count)
        part, clip = slot // clips, lax.rem(slot, clips)

        for mine, group in ((True, ins[:kinds]), (False, ins[kinds:])):
            @pl.when((part == core) == mine)
            def _(out=out, group=group, clip=clip):
                for index, ref in enumerate(group):
                    out[:, index * width:(index + 1) * width] = ref[clip, pl.ds(start, rows), :]


def keep_kernel(c_ref, *refs):
    out = refs[-1]
    kinds = len(refs) // 2
    clips, _, width = refs[0].shape
    core = c_ref[0]
    for part, group in ((core, refs[:kinds]), (1 - core, refs[kinds:2 * kinds])):
        for clip in range(clips):
            for index, ref in enumerate(group):
                out[part * clips + clip, :, index * width:(index + 1) * width] = ref[clip]


def home_kernel(c_ref, back_ref, got_ref, *outs):
    clips, tokens, width = outs[0].shape
    rows = tokens // 2
    core = c_ref[0]
    for clip in range(clips):
        for index, out in enumerate(outs):
            lanes = slice(index * width, (index + 1) * width)
            out[clip, pl.ds(pl.multiple_of(core * rows, rows), rows), :] = back_ref[core * clips + clip, :, lanes]
            out[clip, pl.ds(pl.multiple_of((1 - core) * rows, rows), rows), :] = got_ref[core * clips + clip, :, lanes]


def keys_kernel(heads, z_ref, *refs):
    plane_ref, out = refs
    rows = plane_ref.shape[0]
    window = out.shape[1] - rows
    width = heads * HD
    for head in range(heads):
        for kind in range(4):
            source = slice(kind * width + head * HD, kind * width + (head + 1) * HD)
            lanes = slice((kind % 2) * HD, (kind % 2 + 1) * HD)
            whole_block = plane_ref[:, source]
            for third in range(THIRDS):
                chip = head * THIRDS + third
                if kind < 2:
                    out[chip, 0:rows, lanes] = whole_block
                else:
                    first = third * window
                    count = min(window, rows - first)
                    out[chip, rows:rows + count, lanes] = whole_block[first:first + count]
                    if count < window:
                        out[chip, rows + count:, lanes] = jnp.zeros((window - count, HD), out.dtype)
    for chip in range(heads * THIRDS, out.shape[0]):
        out[chip] = jnp.zeros(out.shape[1:], out.dtype)


def values_pack_kernel(heads, place_ref, *refs):
    ins, out, scr = refs[:-2], refs[-2], refs[-1]
    part = ins[0].shape[0]
    rows = part * len(ins)
    for k, ref in enumerate(ins):
        scr[pl.ds(pl.multiple_of(plane_at(place_ref, -k, len(ins)) * part, part), part), :] = ref[...]
    window = out.shape[1] - 2 * rows
    width = heads * HD
    for head in range(heads):
        for kind in range(3):
            source = slice(kind * width + head * HD, kind * width + (head + 1) * HD)
            whole_block = scr[:, source]
            for third in range(THIRDS):
                chip = head * THIRDS + third
                if kind < 2:
                    out[chip, kind * rows:(kind + 1) * rows, :] = whole_block
                else:
                    first = third * window
                    count = min(window, rows - first)
                    out[chip, 2 * rows:2 * rows + count, :] = whole_block[first:first + count]
                    if count < window:
                        out[chip, 2 * rows + count:, :] = jnp.zeros((window - count, HD), out.dtype)
    for chip in range(heads * THIRDS, out.shape[0]):
        out[chip] = jnp.zeros(out.shape[1:], out.dtype)


def out_unpack_kernel(heads, place_ref, back_ref, *refs):
    outs, scr = refs[:-1], refs[-1]
    part = outs[0].shape[0]
    window = back_ref.shape[1]
    rows = part * len(outs)
    width = heads * HD
    for head in range(heads):
        for kind in range(2):
            lanes = slice(kind * HD, (kind + 1) * HD)
            pieces = [
                back_ref[head * THIRDS + third, 0:min(window, rows - third * window), lanes]
                for third in range(THIRDS)
            ]
            scr[:, kind * width + head * HD:kind * width + (head + 1) * HD] = jnp.concatenate(pieces, axis=0)
    for k, out in enumerate(outs):
        out[...] = scr[pl.ds(pl.multiple_of(plane_at(place_ref, k, len(outs)) * part, part), part), :]


def join_out_kernel(place_ref, *refs):
    ins, own_ref, other_ref = refs[:-2], refs[-2], refs[-1]
    rows, width = ins[0].shape
    clips, width = len(ins) // 2, width // 2
    for k, ref in enumerate(ins):
        slot = plane_at(place_ref, -k, len(ins))
        part, clip = slot // clips, lax.rem(slot, clips)
        for mine, out in ((True, own_ref), (False, other_ref)):
            @pl.when((part == place_ref[1]) == mine)
            def _(ref=ref, out=out, clip=clip):
                for kind in range(2):
                    first = pl.multiple_of((kind * clips + clip) * rows, rows)
                    out[pl.ds(first, rows), :] = ref[:, kind * width:(kind + 1) * width]


def home_out_kernel(c_ref, keep_ref, got_ref, *outs):
    clips, tokens, width = outs[0].shape
    rows = tokens // 2
    core = c_ref[0]
    for ref, half in ((keep_ref, core), (got_ref, 1 - core)):
        for kind, out in enumerate(outs):
            for clip in range(clips):
                first = (kind * clips + clip) * rows
                lanes = pl.ds(pl.multiple_of(core * width, HD), width)
                out[clip, pl.ds(pl.multiple_of(half * rows, rows), rows), :] = ref[first:first + rows, lanes]


def grads_unpack_kernel(heads, z_ref, back_ref, out_ref):
    part = out_ref.shape[1]
    rows = part * out_ref.shape[0]
    window = back_ref.shape[1] - 2 * rows
    width = heads * HD
    for head in range(heads):
        for kind in range(3):
            chips = [head * THIRDS + third for third in range(THIRDS)]
            if kind < 2:
                column = sum(
                    back_ref[chip, kind * rows:(kind + 1) * rows, :].astype(jnp.float32) for chip in chips
                ).astype(jnp.bfloat16)
            else:
                column = jnp.concatenate([
                    back_ref[chip, 2 * rows:2 * rows + min(window, rows - third * window), :]
                    for third, chip in enumerate(chips)
                ], axis=0)
            for d in range(out_ref.shape[0]):
                lanes = slice(kind * width + head * HD, kind * width + (head + 1) * HD)
                out_ref[d, :, lanes] = column[d * part:(d + 1) * part]


def repack(body, name, z, ins, shapes, scratch=(), limit=20 * 2**20):
    shapes = [jax.ShapeDtypeStruct(s, jnp.bfloat16) for s in shapes]
    return kernel_call(body, name, 1, z, [(a, whole(a)) for a in ins], [(s, whole(s)) for s in shapes], list(scratch), limit=limit)


def over_planes(array):
    return lax.all_to_all(array, "z", 0, 0, tiled=True)


def local(queries, keys, values, queries_tan, keys_tan, values_tan, w_out, grad_out):
    w, c = lax.axis_index("w"), lax.axis_index("c")
    z = lax.axis_index("z").astype(jnp.int32).reshape(1)
    core = c.astype(jnp.int32).reshape(1)
    place = jnp.concatenate([z, core])
    clips, tokens, features = queries.shape
    heads = features // HD
    chips = lax.axis_size(("x", "y"))
    slots = 2 * clips
    rows = slots * tokens // 2
    window = pl.cdiv(pl.cdiv(rows, THIRDS), SUB) * SUB

    w_other = swap(w_out, "c")

    far = swap(grad_out, "w")
    near = swap(grad_out, "c")
    kinds = (keys, keys_tan, queries_tan, queries)
    got = tuple(swap(kind, "c") for kind in kinds)
    got_values = tuple(swap(kind, "c") for kind in (values, values_tan))
    half = pl.BlockSpec((clips, tokens // 2, features), lambda i, s: (0, s[0], 0))
    shape = jax.ShapeDtypeStruct((slots, tokens // 2, len(kinds) * features), jnp.bfloat16)
    kept = kernel_call(keep_kernel, "keep_keys", 1, core, [(a, half) for a in kinds + got],
                       [(shape, whole(shape))], [], limit=60 * 2**20)[0]
    plane = over_planes(kept).reshape(rows, -1)
    cross = swap(far, "c")
    width = grad_out.shape[2]
    blocks = [
        lax.dynamic_slice_in_dim(w_out, ((w ^ i) * 2 + (c ^ j)) * width, width, axis=1)
        for i in range(2) for j in range(2)
    ]
    cot = sum(
        jnp.einsum("btf,cf->btc", grad, part, preferred_element_type=jnp.float32)
        for grad, part in zip((grad_out, near, far, cross), blocks)
    ).astype(jnp.bfloat16)
    kinds = (values, values_tan, cot)
    got = got_values + (swap(cot, "c"),)
    shape = (tokens // 2, len(kinds) * features)
    split = repack(split_kernel, "split_values", place, kinds + got, [shape] * slots)
    plane, split = lax.optimization_barrier((plane, split))
    plane_v = along_z(split)

    packed = repack(functools.partial(keys_kernel, heads), "pack_keys", z, [plane], [(chips, rows + window, 2 * HD)])[0]
    recv_k = over_chips(packed)
    recv_k, plane_v = lax.optimization_barrier((recv_k, plane_v))
    other_k = swap(recv_k, "c")
    packed = repack(functools.partial(values_pack_kernel, heads), "pack_values", place, plane_v, [(chips, 2 * rows + window, HD)],
                    [pltpu.VMEM((rows, 3 * features), jnp.bfloat16)])[0]
    recv_v = over_chips(packed)

    probs, weights = attention_weights(z, recv_k, other_k, rows, window)
    recv_v, probs, weights = lax.optimization_barrier((recv_v, probs, weights))
    other_v = swap(recv_v, "c")
    out, dsum = attention_values(z, recv_v, other_v, probs, weights, rows, window)
    back = over_chips(out)
    other_grads, own_half = attention_grads(z, recv_k, other_k, recv_v, other_v, probs, dsum, rows, window)
    back, other_grads = lax.optimization_barrier((back, other_grads))
    shape = (tokens // 2, 2 * features)
    home = along_z(repack(functools.partial(out_unpack_kernel, heads), "unpack_out", place, [back], [shape] * slots,
                          [pltpu.VMEM((rows, 2 * features), jnp.bfloat16)]))
    got = tuple(swap(grad, "c") for grad in other_grads)
    merged = own_half(got)
    home, merged = lax.optimization_barrier((home, merged))
    grads = over_chips(merged)
    own, other = repack(join_out_kernel, "join_out", place, home, [(slots * tokens // 2, features)] * 2)

    def project(chip):
        parts = [
            jnp.dot(rows_of, lax.dynamic_slice_in_dim(weight, chip * 2 * width, 2 * width, axis=1),
                    preferred_element_type=jnp.float32)
            for rows_of, weight in ((own, w_out), (other, w_other))
        ]
        return parts[0] + parts[1]

    got = swap(project(1 - w).astype(jnp.bfloat16), "w")
    total = (project(w) + got.astype(jnp.float32)).astype(jnp.bfloat16)
    outs = repack(home_out_kernel, "home_out", core, [total, swap(total, "c")], [(clips, tokens, width)] * 2)

    shape = (slots, tokens // 2, 3 * features)
    back = over_planes(repack(functools.partial(grads_unpack_kernel, heads), "unpack_grads", z, [grads], [shape])[0])
    grad_k, grad_v, grad_q = repack(home_kernel, "home_grads", core, [back, swap(back, "c")], [queries.shape] * 3)
    return outs[0], outs[1], grad_q, grad_k, grad_v


def solution(mesh):
    seq, tp = ("x", "y", "z"), ("w", "c")
    fine = Mesh(mesh.devices.reshape(4, 4, 4, 2, 2), seq + tp)
    split = P(None, seq, tp)
    return jax.shard_map(
        local,
        mesh=fine,
        in_specs=(split,) * 6 + (P(tp, None), split),
        out_specs=(split,) * 5,
        check_vma=False,
    )
```

```python
import functools

import jax
import jax.numpy as jnp
from jax import lax
from jax.experimental import pallas as pl
from jax.experimental.pallas import tpu as pltpu
from jax.sharding import Mesh, PartitionSpec as P

HD = 128
SCALE = HD ** (-0.5)
LOG2E = 1.4426950408889634
SUB = 16
W_GROUP, W_UNROLL = 4, 4
V_GROUP = 8
G_GROUP = 16
VMEM_LIMIT = 52 * 2**20
NT = (((1,), (1,)), ((), ()))
NN = (((1,), (0,)), ((), ()))


def dot(a, b, dims=NN):
    return lax.dot_general(a, b, dims, preferred_element_type=jnp.float32)


def piece(ref, j, group, first, count, lanes=slice(None)):
    block = ref[pl.ds(j * group, group), first:first + count, lanes]
    return block.reshape(group * count, block.shape[-1])


def key_rows(half, j, group, blocks, rows):
    start = (half * blocks + j * group) * rows
    return pl.ds(pl.multiple_of(start, group * rows), group * rows)


def weights_kernel(rows, z_ref, q_ref, ka_ref, kb_ref, p_ref, w_ref, s_scr, t_scr):
    blocks = ka_ref.shape[0]
    tile = p_ref.shape[1]
    qtq = q_ref[...].reshape(tile, 2 * HD)
    q = qtq[:, HD:]

    top = jnp.full((1, tile), -jnp.inf, jnp.float32)
    for half, ref in enumerate((ka_ref, kb_ref)):
        def scores(j, top, half=half, ref=ref):
            here = key_rows(half, j, W_GROUP, blocks, rows)
            both = piece(ref, j, W_GROUP, 0, rows)
            s = dot(both[:, :HD], q, NT)
            s_scr[here, :] = s
            t_scr[here, :] = dot(both, qtq, NT)
            return jnp.maximum(top, jnp.max(s, axis=0, keepdims=True))
        top = lax.fori_loop(0, blocks // W_GROUP, scores, top, unroll=W_UNROLL)

    zero = jnp.zeros((1, tile), jnp.float32)

    def sums(j, carry):
        total, slope = carry
        here = key_rows(0, j, W_GROUP, blocks, rows)
        e = jnp.exp2((s_scr[here, :] - top) * (SCALE * LOG2E))
        s_scr[here, :] = e
        total += jnp.sum(e, axis=0, keepdims=True)
        slope += jnp.sum(e * t_scr[here, :], axis=0, keepdims=True)
        return total, slope

    total, slope = lax.fori_loop(0, 2 * blocks // W_GROUP, sums, (zero, zero), unroll=W_UNROLL)
    inv = 1.0 / total
    slope = slope * inv

    def store(j, carry):
        here = key_rows(0, j, W_GROUP, blocks, rows)
        p = s_scr[here, :] * inv
        p_ref[here, :] = p.astype(jnp.bfloat16)
        w_ref[here, :] = (p * (t_scr[here, :] - slope)).astype(jnp.bfloat16)
        return carry

    lax.fori_loop(0, 2 * blocks // W_GROUP, store, 0, unroll=W_UNROLL)


def window_rows(refs):
    return jnp.concatenate([ref[...].reshape(-1, HD) for ref in refs], axis=0)


def put_rows(ref, lanes, value, first=0):
    blocks, height, _ = ref.shape
    tile = blocks * SUB
    for i in range((height - first) // SUB):
        ref[:, first + i * SUB:first + (i + 1) * SUB, lanes] = value[i * tile:(i + 1) * tile].astype(ref.dtype).reshape(blocks, SUB, HD)


def values_kernel(last, z_ref, v_ref, t_ref, p_ref, w_ref, *refs):
    step = pl.program_id(0)
    if last:
        *g_refs, start_ref, out_ref, d_ref, acc = refs
    else:
        acc = refs[0]
    chunk = p_ref.shape[0]
    v = v_ref[...].reshape(chunk, HD)
    both = jnp.concatenate([v, t_ref[...].reshape(chunk, HD)], axis=1).T

    @pl.when(step == 0)
    def _():
        acc[...] = start_ref[...] if last else jnp.zeros_like(acc)

    acc[0:2 * HD, :] += dot(both, p_ref[...])
    acc[2 * HD:, :] += dot(both[0:HD], w_ref[...])

    if last:
        @pl.when(step == pl.num_programs(0) - 1)
        def _():
            g = window_rows(g_refs).astype(jnp.float32)
            attn = acc[0:HD, :].T.astype(jnp.bfloat16)
            rounded = acc[0:HD, :].astype(jnp.bfloat16).astype(jnp.float32)
            d_ref[...] = jnp.sum(rounded * g.T, axis=0, keepdims=True)
            tan = acc[HD:2 * HD, :] + SCALE * acc[2 * HD:, :]
            put_rows(out_ref, slice(0, HD), attn)
            put_rows(out_ref, slice(HD, 2 * HD), tan.T)


def grads_kernel(last, z_ref, k_ref, v_ref, p_ref, d_ref, *refs):
    step = pl.program_id(0)
    chunk, queries = p_ref.shape
    count = (len(refs) - (5 if last else 3)) // 2
    q, g, refs = window_rows(refs[:count]), window_rows(refs[count:2 * count]), refs[2 * count:]
    if last:
        start_ref, got_k_ref, got_v_ref, out_ref, acc = refs
    else:
        dk_ref, dv_ref, acc = refs
    k = k_ref[...].reshape(chunk, HD)
    v = v_ref[...].reshape(chunk, HD)
    p = p_ref[...]

    @pl.when(step == 0)
    def _():
        acc[...] = start_ref[...] if last else jnp.zeros_like(acc)

    ds = (p.astype(jnp.float32) * (dot(v, g, NT) - d_ref[...])).astype(jnp.bfloat16)
    dk = (SCALE * dot(ds, q)).reshape(k_ref.shape)
    dv = dot(p, g).reshape(k_ref.shape)
    acc[...] += dot(k.T, ds)

    if last:
        blocks, rows, _ = k_ref.shape
        group = pl.ds(step * blocks, blocks)
        out_ref[group, 0:rows, :] = (dk + got_k_ref[...].astype(jnp.float32)).astype(jnp.bfloat16)
        out_ref[group, rows:2 * rows, :] = (dv + got_v_ref[...].astype(jnp.float32)).astype(jnp.bfloat16)

        @pl.when(step == pl.num_programs(0) - 1)
        def _():
            put_rows(out_ref, slice(0, HD), (SCALE * acc[...]).T, 2 * rows)
    else:
        dk_ref[...] = dk.astype(jnp.bfloat16)
        dv_ref[...] = dv.astype(jnp.bfloat16)


def whole(array):
    return pl.BlockSpec(array.shape, lambda i, s: (0,) * len(array.shape))


def kernel_call(body, name, grid, scalars, ins, outs, scratch, flops=0, bytes_accessed=4 * 2**20, limit=VMEM_LIMIT):
    arrays, in_specs = zip(*ins)
    shapes, out_specs = zip(*outs)
    return pl.pallas_call(
        body,
        grid_spec=pltpu.PrefetchScalarGridSpec(
            num_scalar_prefetch=1,
            grid=(grid,),
            in_specs=list(in_specs),
            out_specs=list(out_specs),
            scratch_shapes=scratch,
        ),
        out_shape=list(shapes),
        name=name,
        compiler_params=pltpu.CompilerParams(vmem_limit_bytes=limit),
        cost_estimate=pl.CostEstimate(flops=flops, bytes_accessed=bytes_accessed, transcendentals=0),
    )(scalars, *arrays)


def specs(blocks, rows, window):
    tile = blocks * SUB
    keys = 2 * blocks * rows
    q_spec = pl.BlockSpec((blocks, SUB, 2 * HD), lambda i, s: (0, rows // SUB + i, 0))
    g_spec = pl.BlockSpec((blocks, SUB, HD), lambda i, s: (0, 2 * rows // SUB + i, 0))
    p_spec = pl.BlockSpec((keys, tile), lambda i, s: (0, i))
    d_spec = pl.BlockSpec((1, tile), lambda i, s: (0, i))
    return q_spec, g_spec, p_spec, d_spec, keys, tile, window // SUB


def attention_weights(z, recv_k, other_k, rows, window):
    q_spec, _, p_spec, _, keys, tile, grid = specs(recv_k.shape[0], rows, window)
    p_shape = jax.ShapeDtypeStruct((keys, grid * tile), jnp.bfloat16)
    return kernel_call(
        functools.partial(weights_kernel, rows), "weights", grid, z,
        [(recv_k, q_spec), (recv_k, whole(recv_k)), (other_k, whole(other_k))],
        [(p_shape, p_spec), (p_shape, p_spec)],
        [pltpu.VMEM((keys, tile), jnp.float32), pltpu.VMEM((keys, tile), jnp.float32)],
        8 * keys * grid * tile * HD, 32 * 2**20)


def windows(array, first, window, lane):
    blocks = array.shape[0]
    return [
        (array, pl.BlockSpec((blocks, SUB, HD), lambda i, s, at=first // SUB + part: (0, at, lane)))
        for part in range(window // SUB)
    ]


def attention_values(z, recv_v, other_v, probs, weights, rows, window):
    blocks = recv_v.shape[0]
    keys, queries = probs.shape
    half = blocks // V_GROUP
    sums = jax.ShapeDtypeStruct((3 * HD, queries), jnp.float32)
    out_shape = jax.ShapeDtypeStruct((blocks, window, 2 * HD), jnp.bfloat16)
    d_shape = jax.ShapeDtypeStruct((1, queries), jnp.float32)

    def ins(array, first):
        p_spec = pl.BlockSpec((V_GROUP * rows, queries), lambda i, s: (first + i, 0))
        return [
            (array, pl.BlockSpec((V_GROUP, rows, HD), lambda i, s: (i, 0, 0))),
            (array, pl.BlockSpec((V_GROUP, rows, HD), lambda i, s: (i, 1, 0))),
            (probs, p_spec), (weights, p_spec),
        ]

    start = kernel_call(
        functools.partial(values_kernel, False), "values_own", half, z, ins(recv_v, 0),
        [(sums, whole(sums))], [], 3 * keys * queries * HD, 8 * 2**20)[0]
    g = windows(recv_v, 2 * rows, window, 0)
    return kernel_call(
        functools.partial(values_kernel, True), "values_other", half, z,
        ins(other_v, half) + g + [(start, whole(start))],
        [(out_shape, whole(out_shape)), (d_shape, whole(d_shape))],
        [pltpu.VMEM(sums.shape, sums.dtype)], 3 * keys * queries * HD, 8 * 2**20)


def attention_grads(z, recv_k, other_k, recv_v, other_v, probs, dsum, rows, window):
    blocks = recv_v.shape[0]
    keys, queries = probs.shape
    half = blocks // G_GROUP
    shape = jax.ShapeDtypeStruct((blocks, rows, HD), jnp.bfloat16)
    merged = jax.ShapeDtypeStruct((blocks, 2 * rows + window, HD), jnp.bfloat16)
    sums = jax.ShapeDtypeStruct((HD, queries), jnp.float32)
    block = pl.BlockSpec((G_GROUP, rows, HD), lambda i, s: (i, 0, 0))

    def ins(k, v, first):
        return [
            (k, block), (v, block),
            (probs, pl.BlockSpec((G_GROUP * rows, queries), lambda i, s: (first + i, 0))),
            (dsum, whole(dsum)),
        ] + windows(recv_k, rows, window, 1) + windows(recv_v, 2 * rows, window, 0)

    other_dk, other_dv, start = kernel_call(
        functools.partial(grads_kernel, False), "grads_other", half, z, ins(other_k, other_v, half),
        [(shape, block), (shape, block), (sums, whole(sums))], [], 5 * keys * queries * HD, 8 * 2**20)

    def own(got):
        return kernel_call(
            functools.partial(grads_kernel, True), "grads_own", half, z,
            ins(recv_k, recv_v, 0) + [(start, whole(start)), (got[0], block), (got[1], block)],
            [(merged, whole(merged))], [pltpu.VMEM(sums.shape, sums.dtype)], 5 * keys * queries * HD, 8 * 2**20)[0]

    return (other_dk, other_dv), own


THIRDS = 3
SWAP = [(0, 1), (1, 0)]


def swap(array, axis):
    return lax.ppermute(array, axis, SWAP)


def along_z(pieces):
    count = len(pieces)
    routes = [[(i, (i + k) % count) for i in range(count)] for k in range(count)]
    return [pieces[0]] + [lax.ppermute(a, "z", route) for a, route in zip(pieces[1:], routes[1:])]


def over_chips(array):
    return lax.all_to_all(array, ("x", "y"), 0, 0, tiled=True)


def plane_at(place_ref, shift, count):
    return lax.rem(place_ref[0] + shift + count, count)


def split_kernel(place_ref, *refs):
    count = 4
    ins, outs = refs[:-count], refs[-count:]
    kinds = len(ins) // 2
    clips, tokens, width = ins[0].shape
    rows = tokens // 2
    core = place_ref[1]
    start = pl.multiple_of(core * rows, rows)
    for k, out in enumerate(outs):
        slot = plane_at(place_ref, k, count)
        part, clip = slot // clips, lax.rem(slot, clips)

        for mine, group in ((True, ins[:kinds]), (False, ins[kinds:])):
            @pl.when((part == core) == mine)
            def _(out=out, group=group, clip=clip):
                for index, ref in enumerate(group):
                    out[:, index * width:(index + 1) * width] = ref[clip, pl.ds(start, rows), :]


def keep_kernel(c_ref, *refs):
    out = refs[-1]
    kinds = len(refs) // 2
    clips, _, width = refs[0].shape
    core = c_ref[0]
    for part, group in ((core, refs[:kinds]), (1 - core, refs[kinds:2 * kinds])):
        for clip in range(clips):
            for index, ref in enumerate(group):
                out[part * clips + clip, :, index * width:(index + 1) * width] = ref[clip]


def home_kernel(c_ref, back_ref, got_ref, *outs):
    clips, tokens, width = outs[0].shape
    rows = tokens // 2
    core = c_ref[0]
    for clip in range(clips):
        for index, out in enumerate(outs):
            lanes = slice(index * width, (index + 1) * width)
            out[clip, pl.ds(pl.multiple_of(core * rows, rows), rows), :] = back_ref[core * clips + clip, :, lanes]
            out[clip, pl.ds(pl.multiple_of((1 - core) * rows, rows), rows), :] = got_ref[core * clips + clip, :, lanes]


def keys_kernel(heads, z_ref, *refs):
    plane_ref, out = refs
    rows = plane_ref.shape[0]
    window = out.shape[1] - rows
    width = heads * HD
    for head in range(heads):
        for kind in range(4):
            source = slice(kind * width + head * HD, kind * width + (head + 1) * HD)
            lanes = slice((kind % 2) * HD, (kind % 2 + 1) * HD)
            whole_block = plane_ref[:, source]
            for third in range(THIRDS):
                chip = head * THIRDS + third
                if kind < 2:
                    out[chip, 0:rows, lanes] = whole_block
                else:
                    first = third * window
                    count = min(window, rows - first)
                    out[chip, rows:rows + count, lanes] = whole_block[first:first + count]
                    if count < window:
                        out[chip, rows + count:, lanes] = jnp.zeros((window - count, HD), out.dtype)
    for chip in range(heads * THIRDS, out.shape[0]):
        out[chip] = jnp.zeros(out.shape[1:], out.dtype)


def values_pack_kernel(heads, place_ref, *refs):
    ins, out, scr = refs[:-2], refs[-2], refs[-1]
    part = ins[0].shape[0]
    rows = part * len(ins)
    for k, ref in enumerate(ins):
        scr[pl.ds(pl.multiple_of(plane_at(place_ref, -k, len(ins)) * part, part), part), :] = ref[...]
    window = out.shape[1] - 2 * rows
    width = heads * HD
    for head in range(heads):
        for kind in range(3):
            source = slice(kind * width + head * HD, kind * width + (head + 1) * HD)
            whole_block = scr[:, source]
            for third in range(THIRDS):
                chip = head * THIRDS + third
                if kind < 2:
                    out[chip, kind * rows:(kind + 1) * rows, :] = whole_block
                else:
                    first = third * window
                    count = min(window, rows - first)
                    out[chip, 2 * rows:2 * rows + count, :] = whole_block[first:first + count]
                    if count < window:
                        out[chip, 2 * rows + count:, :] = jnp.zeros((window - count, HD), out.dtype)
    for chip in range(heads * THIRDS, out.shape[0]):
        out[chip] = jnp.zeros(out.shape[1:], out.dtype)


def out_unpack_kernel(heads, place_ref, back_ref, *refs):
    outs, scr = refs[:-1], refs[-1]
    part = outs[0].shape[0]
    window = back_ref.shape[1]
    rows = part * len(outs)
    width = heads * HD
    for head in range(heads):
        for kind in range(2):
            lanes = slice(kind * HD, (kind + 1) * HD)
            pieces = [
                back_ref[head * THIRDS + third, 0:min(window, rows - third * window), lanes]
                for third in range(THIRDS)
            ]
            scr[:, kind * width + head * HD:kind * width + (head + 1) * HD] = jnp.concatenate(pieces, axis=0)
    for k, out in enumerate(outs):
        out[...] = scr[pl.ds(pl.multiple_of(plane_at(place_ref, k, len(outs)) * part, part), part), :]


def join_out_kernel(place_ref, *refs):
    ins, own_ref, other_ref = refs[:-2], refs[-2], refs[-1]
    rows, width = ins[0].shape
    clips, width = len(ins) // 2, width // 2
    for k, ref in enumerate(ins):
        slot = plane_at(place_ref, -k, len(ins))
        part, clip = slot // clips, lax.rem(slot, clips)
        for mine, out in ((True, own_ref), (False, other_ref)):
            @pl.when((part == place_ref[1]) == mine)
            def _(ref=ref, out=out, clip=clip):
                for kind in range(2):
                    first = pl.multiple_of((kind * clips + clip) * rows, rows)
                    out[pl.ds(first, rows), :] = ref[:, kind * width:(kind + 1) * width]


def home_out_kernel(c_ref, keep_ref, got_ref, *outs):
    clips, tokens, width = outs[0].shape
    rows = tokens // 2
    core = c_ref[0]
    for ref, half in ((keep_ref, core), (got_ref, 1 - core)):
        for kind, out in enumerate(outs):
            for clip in range(clips):
                first = (kind * clips + clip) * rows
                lanes = pl.ds(pl.multiple_of(core * width, HD), width)
                out[clip, pl.ds(pl.multiple_of(half * rows, rows), rows), :] = ref[first:first + rows, lanes]


def grads_unpack_kernel(heads, z_ref, back_ref, out_ref):
    part = out_ref.shape[1]
    rows = part * out_ref.shape[0]
    window = back_ref.shape[1] - 2 * rows
    width = heads * HD
    for head in range(heads):
        for kind in range(3):
            chips = [head * THIRDS + third for third in range(THIRDS)]
            if kind < 2:
                column = sum(
                    back_ref[chip, kind * rows:(kind + 1) * rows, :].astype(jnp.float32) for chip in chips
                ).astype(jnp.bfloat16)
            else:
                column = jnp.concatenate([
                    back_ref[chip, 2 * rows:2 * rows + min(window, rows - third * window), :]
                    for third, chip in enumerate(chips)
                ], axis=0)
            for d in range(out_ref.shape[0]):
                lanes = slice(kind * width + head * HD, kind * width + (head + 1) * HD)
                out_ref[d, :, lanes] = column[d * part:(d + 1) * part]


def repack(body, name, z, ins, shapes, scratch=(), limit=20 * 2**20):
    shapes = [jax.ShapeDtypeStruct(s, jnp.bfloat16) for s in shapes]
    return kernel_call(body, name, 1, z, [(a, whole(a)) for a in ins], [(s, whole(s)) for s in shapes], list(scratch), limit=limit)


def over_planes(array):
    return lax.all_to_all(array, "z", 0, 0, tiled=True)


def local(queries, keys, values, queries_tan, keys_tan, values_tan, w_out, grad_out):
    w, c = lax.axis_index("w"), lax.axis_index("c")
    z = lax.axis_index("z").astype(jnp.int32).reshape(1)
    core = c.astype(jnp.int32).reshape(1)
    place = jnp.concatenate([z, core])
    clips, tokens, features = queries.shape
    heads = features // HD
    chips = lax.axis_size(("x", "y"))
    slots = 2 * clips
    rows = slots * tokens // 2
    window = pl.cdiv(pl.cdiv(rows, THIRDS), SUB) * SUB

    w_other = swap(w_out, "c")

    far = swap(grad_out, "w")
    near = swap(grad_out, "c")
    kinds = (keys, keys_tan, queries_tan, queries)
    got = tuple(swap(kind, "c") for kind in kinds)
    got_values = tuple(swap(kind, "c") for kind in (values, values_tan))
    half = pl.BlockSpec((clips, tokens // 2, features), lambda i, s: (0, s[0], 0))
    shape = jax.ShapeDtypeStruct((slots, tokens // 2, len(kinds) * features), jnp.bfloat16)
    kept = kernel_call(keep_kernel, "keep_keys", 1, core, [(a, half) for a in kinds + got],
                       [(shape, whole(shape))], [], limit=60 * 2**20)[0]
    plane = over_planes(kept).reshape(rows, -1)
    cross = swap(far, "c")
    width = grad_out.shape[2]
    blocks = [
        lax.dynamic_slice_in_dim(w_out, ((w ^ i) * 2 + (c ^ j)) * width, width, axis=1)
        for i in range(2) for j in range(2)
    ]
    cot = sum(
        jnp.einsum("btf,cf->btc", grad, part, preferred_element_type=jnp.float32)
        for grad, part in zip((grad_out, near, far, cross), blocks)
    ).astype(jnp.bfloat16)
    kinds = (values, values_tan, cot)
    got = got_values + (swap(cot, "c"),)
    shape = (tokens // 2, len(kinds) * features)
    split = repack(split_kernel, "split_values", place, kinds + got, [shape] * slots)
    plane, split = lax.optimization_barrier((plane, split))
    plane_v = along_z(split)

    packed = repack(functools.partial(keys_kernel, heads), "pack_keys", z, [plane], [(chips, rows + window, 2 * HD)])[0]
    recv_k = over_chips(packed)
    recv_k, plane_v = lax.optimization_barrier((recv_k, plane_v))
    other_k = swap(recv_k, "c")
    packed = repack(functools.partial(values_pack_kernel, heads), "pack_values", place, plane_v, [(chips, 2 * rows + window, HD)],
                    [pltpu.VMEM((rows, 3 * features), jnp.bfloat16)])[0]
    recv_v = over_chips(packed)

    probs, weights = attention_weights(z, recv_k, other_k, rows, window)
    recv_v, probs, weights = lax.optimization_barrier((recv_v, probs, weights))
    other_v = swap(recv_v, "c")
    out, dsum = attention_values(z, recv_v, other_v, probs, weights, rows, window)
    back = over_chips(out)
    other_grads, own_half = attention_grads(z, recv_k, other_k, recv_v, other_v, probs, dsum, rows, window)
    back, other_grads = lax.optimization_barrier((back, other_grads))
    shape = (tokens // 2, 2 * features)
    home = along_z(repack(functools.partial(out_unpack_kernel, heads), "unpack_out", place, [back], [shape] * slots,
                          [pltpu.VMEM((rows, 2 * features), jnp.bfloat16)]))
    got = tuple(swap(grad, "c") for grad in other_grads)
    merged = own_half(got)
    home, merged = lax.optimization_barrier((home, merged))
    grads = over_chips(merged)
    own, other = repack(join_out_kernel, "join_out", place, home, [(slots * tokens // 2, features)] * 2)

    def project(chip):
        parts = [
            jnp.dot(rows_of, lax.dynamic_slice_in_dim(weight, chip * 2 * width, 2 * width, axis=1),
                    preferred_element_type=jnp.float32)
            for rows_of, weight in ((own, w_out), (other, w_other))
        ]
        return parts[0] + parts[1]

    got = swap(project(1 - w).astype(jnp.bfloat16), "w")
    total = (project(w) + got.astype(jnp.float32)).astype(jnp.bfloat16)
    outs = repack(home_out_kernel, "home_out", core, [total, swap(total, "c")], [(clips, tokens, width)] * 2)

    shape = (slots, tokens // 2, 3 * features)
    back = over_planes(repack(functools.partial(grads_unpack_kernel, heads), "unpack_grads", z, [grads], [shape])[0])
    grad_k, grad_v, grad_q = repack(home_kernel, "home_grads", core, [back, swap(back, "c")], [queries.shape] * 3)
    return outs[0], outs[1], grad_q, grad_k, grad_v


def solution(mesh):
    seq, tp = ("x", "y", "z"), ("w", "c")
    fine = Mesh(mesh.devices.reshape(4, 4, 4, 2, 2), seq + tp)
    split = P(None, seq, tp)
    return jax.shard_map(
        local,
        mesh=fine,
        in_specs=(split,) * 6 + (P(tp, None), split),
        out_specs=(split,) * 5,
        check_vma=False,
    )
```
